128 devices in a mesh: dp: 16 (over z_hi, y, core), tensor: 8 (over x, z_lo).
Axes of the slice: x: 4, y: 4, z: 4 (z_hi: 2, z_lo: 2; z = z_hi * 2 + z_lo), core: 2. Of those that a mesh axis runs over, the one named last changes fastest.
Arguments:
- hidden_in: bfloat16 [16384, 4096], P(('dp', 'tensor')), may hold values from -500 to 500
- teacher: bfloat16 [16384, 4096], P(('dp', 'tensor')), may hold values from -3 to 3
- row_source: int32 [16384], P(('dp', 'tensor')), may hold values from 0 to 16383, as said below
- segments: int32 [16, 1024], P('dp'), may hold values from 0 to 3, never falling along the last dimension, each value on 1 to 512 neighbouring positions
- branch: bfloat16 [16384, 4096], P(('dp', 'tensor')), may hold values from -3 to 3
- queries: bfloat16 [16384, 4096], P('dp', 'tensor'), may hold values from -6 to 6
- key_rot: bfloat16 [16384, 1024], P('dp', 'tensor'), may hold values from -4 to 4
- value_rows: bfloat16 [16384, 1024], P('dp', 'tensor'), may hold values from -5 to 5
- attended: bfloat16 [16384, 4096], P('dp', 'tensor'), may hold values from -5 to 5
- norm_gain: float32 [4096], replicated, may hold values from 0.1 to 1.9
- w_query: bfloat16 [4096, 4096], P(None, 'tensor'), may hold values from -0.09375 to 0.09375
- w_key: bfloat16 [4096, 1024], P(None, 'tensor'), may hold values from -0.09375 to 0.09375
- w_value: bfloat16 [4096, 1024], P(None, 'tensor'), may hold values from -0.09375 to 0.09375
- w_out: bfloat16 [4096, 4096], P('tensor'), may hold values from -0.09375 to 0.09375
Outputs:
- grad_query: float32 [4096, 4096], P('dp', 'tensor')
- grad_key: float32 [4096, 1024], P('dp', 'tensor')
- grad_value: float32 [4096, 1024], P('dp', 'tensor')
- grad_out: float32 [4096, 4096], P('tensor', 'dp')
- grad_gain: float32 [4096], replicated
- d_hidden_in: float32 [16384, 4096], P(('dp', 'tensor'))
The draws below stay inside these ranges and needn't reach their ends.
Inputs may be any that keep to these rules, and one draw needn't show every extreme that they name: Student row g takes teacher row row_source[g]; each teacher row is taken once; the teacher row lies on a device of the same tensor index as row g. Of one device's teacher rows at most 9 go to any one device, and in every draw some device sends exactly 9 to some device.
All inputs are finite; a program needn't handle non-finite values.
Results may differ from the reference program's by a relative error of at most 0.018.
Values may be sent and summed in bfloat16 or wider, within the bound.
A program may use at most 192 MiB of HBM per device.

```python
import math
import jax
import jax.numpy as jnp
import numpy as np
from jax import lax

D = 4096
HEADS = 32
KVH = 8
HD = 128
TOK_GRP = 1024
DOCS = 4
TOKENS = 16384
N_DP = 16
N_TENSOR = 8


def draw_hidden_in(key, part):
    key = jax.random.fold_in(key, 1)
    keys = jax.random.split(key, 3)
    col_scale = jnp.exp(jax.random.uniform(keys[1], (1, D), jnp.float32, 0.0, math.log(10.0)))
    row_scale = jnp.exp(jax.random.uniform(keys[0], (TOKENS, 1), jnp.float32, 0.0, math.log(10.0)))
    base = jax.random.truncated_normal(keys[2], -4.0, 4.0, (TOKENS, D), jnp.float32)
    return (base * row_scale * col_scale).astype(jnp.bfloat16)


def draw_queries(key, part):
    key = jax.random.fold_in(key, 5)
    keys = jax.random.split(key, 1)
    return jax.random.truncated_normal(keys[0], -4.0, 4.0, (TOKENS, HEADS * HD), jnp.float32).astype(jnp.bfloat16)


def draw_key_rot(key, part):
    key = jax.random.fold_in(key, 6)
    keys = jax.random.split(key, 1)
    return jax.random.truncated_normal(keys[0], -4.0, 4.0, (TOKENS, KVH * HD), jnp.float32).astype(jnp.bfloat16)


def draw_row_source(key, part):
    key = jax.random.fold_in(key, 4)
    per_device = TOK_GRP // N_TENSOR
    whole = per_device // N_DP
    rest = per_device % N_DP
    keys = jax.random.split(key, 3)
    peer_ids = jnp.arange(N_DP, dtype=jnp.int32)
    counts = whole + jnp.logical_and(peer_ids >= 1, peer_ids < rest).astype(jnp.int32) + (peer_ids == 0).astype(jnp.int32) - jnp.logical_and(peer_ids == N_DP - 1, rest == 0).astype(jnp.int32)
    bounds = jnp.cumsum(counts)
    rounds = jnp.arange(per_device, dtype=jnp.int32)
    which = jnp.sum((rounds[:, None] >= bounds[None, :]).astype(jnp.int32), axis=1)
    offset_perms = jax.vmap(lambda single: jax.random.permutation(single, N_DP))(jax.random.split(keys[0], N_TENSOR))
    offsets = offset_perms[:, which].astype(jnp.int32)
    slot_round = jax.vmap(lambda single: jax.random.permutation(single, per_device))(jax.random.split(keys[1], N_TENSOR * N_DP)).reshape(N_TENSOR, N_DP, per_device).astype(jnp.int32)
    row_pick = jax.vmap(lambda single: jax.random.permutation(single, per_device))(jax.random.split(keys[2], N_TENSOR * N_DP)).reshape(N_TENSOR, N_DP, per_device).astype(jnp.int32)
    tensor_ids = jnp.arange(N_TENSOR, dtype=jnp.int32)[:, None, None]
    dest_ids = jnp.arange(N_DP, dtype=jnp.int32)[None, :, None]
    offsets_full = jnp.broadcast_to(offsets[:, None, :], (N_TENSOR, N_DP, per_device))
    offset_of = jnp.take_along_axis(offsets_full, slot_round, axis=2)
    source = (dest_ids + offset_of) % N_DP
    local_row = row_pick[tensor_ids, source, slot_round]
    teacher_row = (source * N_TENSOR + tensor_ids) * per_device + local_row
    return jnp.transpose(teacher_row, (1, 0, 2)).reshape(TOKENS).astype(jnp.int32)


def block_scale(own_key, extent, shards, low, high):
    level, own = 1.0, jax.random.fold_in(own_key, 6)
    for position, blocks in shards:
        draws = jnp.exp(jax.random.uniform(jax.random.fold_in(own, position), (blocks,), jnp.float32, low / len(shards), high / len(shards)))
        level = level * jnp.repeat(draws, extent[position] // blocks).reshape([-1 if axis == position else 1 for axis in range(len(extent))])
    return level


def profile(count, total, limit, skew):
    weights = [(1 << 20) // math.isqrt(grade ** skew) + 1 for grade in range(2, count + 1)]
    spare, given = total - limit - (count - 1), [1] * (count - 1)
    while spare > 0:
        free = [i for i in range(count - 1) if given[i] < limit]
        mass, remaining = sum([weights[i] for i in free]), spare
        for i in free:
            more = min(limit - given[i], max(1, remaining * weights[i] // mass), spare)
            given[i] = given[i] + more
            spare = spare - more
    return np.array([limit] + given)


def uneven_parts(own_key, count, total, most, lean):
    if count == 2:
        one = jax.random.randint(own_key, (), max(1, total - most), min(most, total - 1) + 1)
        return jnp.stack([one, total - one])
    lengths = jnp.asarray(profile(count, total, most, lean), jnp.int32)
    couples = (count - 1) // 2
    donor, sink = lengths[1:1 + 2 * couples:2], lengths[2:2 + 2 * couples:2]
    slack = jnp.minimum(donor - 1, most - sink)
    moved = jax.random.randint(jax.random.fold_in(own_key, 1), (couples,), 0, 1 << 20) % (slack + 1)
    lengths = lengths.at[1:1 + 2 * couples:2].set(donor - moved).at[2:2 + 2 * couples:2].set(sink + moved)
    return lengths[jax.random.permutation(jax.random.fold_in(own_key, 2), count)]


def centred(key, dims, width, limit, pieces=(), kind=jnp.bfloat16):
    values = jax.random.normal(key, dims, jnp.float32) * width
    if len(pieces) > 0:
        values = block_scale(key, dims, pieces, -0.22, 0.18) * values
    return jnp.clip(values, min=-limit, max=limit).astype(kind)


def setup_inputs(seed: int = 0) -> dict:
    key_of = jax.random.split(jax.random.key(seed), 15)
    return {
        "hidden_in": draw_hidden_in(jax.random.fold_in(key_of[14], 71), 0),
        "teacher": centred(key_of[1], (TOKENS, D), 0.5, 3.0, ((0, 128),)),
        "row_source": draw_row_source(jax.random.fold_in(key_of[14], 71), 0),
        "segments": jax.vmap(lambda own: jnp.searchsorted(jnp.cumsum(uneven_parts(own, DOCS, TOK_GRP, TOK_GRP // 2, 2)), jnp.arange(TOK_GRP), side="right"))(jax.random.split(key_of[3], N_DP)).reshape((N_DP, TOK_GRP)).astype(jnp.int32),
        "branch": centred(key_of[4], (TOKENS, D), 0.5, 3.0, ((0, 128),)),
        "queries": draw_queries(jax.random.fold_in(key_of[14], 71), 0),
        "key_rot": draw_key_rot(jax.random.fold_in(key_of[14], 71), 0),
        "value_rows": centred(key_of[7], (TOKENS, KVH * HD), 1.0, 5.0, ((0, 16), (1, 8))),
        "attended": centred(key_of[8], (TOKENS, HEADS * HD), 1.0, 5.0, ((0, 16), (1, 8))),
        "norm_gain": jnp.clip(1.0 + 0.18 * jax.random.normal(key_of[9], (D,), jnp.float32), 0.1, 1.9),
        "w_query": centred(key_of[10], (D, HEADS * HD), D ** -0.5, 0.09375, ((1, 8),)),
        "w_key": centred(key_of[11], (D, KVH * HD), D ** -0.5, 0.09375, ((1, 8),)),
        "w_value": centred(key_of[12], (D, KVH * HD), D ** -0.5, 0.09375, ((1, 8),)),
        "w_out": centred(key_of[13], (HEADS * HD, D), (HEADS * HD) ** -0.5, 0.09375, ((0, 8),)),
    }


theta_base = 500000.0
eps_norm = 1e-05

def rounded(values):
    return lax.optimization_barrier(values.astype(jnp.bfloat16)).astype(jnp.float32)

def segment_positions(segment_ids):
    row_index = jnp.arange(segment_ids.shape[0], dtype=jnp.int32)
    before = lax.optimization_barrier(jnp.sum((segment_ids[None, :] < segment_ids[:, None]).astype(jnp.int32), axis=1))
    return row_index - before

def rotation_tables(positions):
    half_dim = HD // 2
    frequency = theta_base ** (-2.0 * jnp.arange(half_dim, dtype=jnp.float32) / HD)
    angles = positions.astype(jnp.float32)[:, None] * frequency[None, :]
    return (jnp.cos(angles), jnp.sin(angles))

def unrotate(values, cos_table, sin_table):
    half_dim = values.shape[-1] // 2
    first_half = values[..., :half_dim]
    second = values[..., half_dim:]
    cosine = cos_table[:, None, :]
    sine_part = sin_table[:, None, :]
    return jnp.concatenate([first_half * cosine + second * sine_part, second * cosine - first_half * sine_part], axis=-1)

def group_terms(rows_in, target, branch, queries, key_rot, value_rows, attended, segment_ids, norm_gain, w_query, w_key, w_value, w_out):
    f32 = jnp.float32
    bf16 = jnp.bfloat16
    row_count = rows_in.shape[0]
    group_size = HEADS // KVH
    scale = HD ** (-0.5)
    floated = rows_in.astype(f32)
    inv_rms = lax.rsqrt(lax.optimization_barrier(jnp.mean(floated * floated, axis=1, keepdims=True)) + eps_norm)
    unit_rows = floated * inv_rms
    normed = (unit_rows * norm_gain[None, :]).astype(bf16)
    cos_table, sin_table = rotation_tables(segment_positions(segment_ids))
    grouped = queries.reshape(row_count, KVH, group_size, HD)
    keys_three = key_rot.reshape(row_count, KVH, HD)
    values_three = value_rows.reshape(row_count, KVH, HD)
    row_index = jnp.arange(row_count, dtype=jnp.int32)
    allowed = (segment_ids[:, None] == segment_ids[None, :]) & (row_index[None, :] <= row_index[:, None])
    scores = jnp.einsum('qkgd,ckd->kgqc', grouped.astype(f32), keys_three.astype(f32)) * scale
    scores = jnp.where(allowed, scores, -1e+30)
    row_max = lax.optimization_barrier(jnp.max(scores, axis=-1, keepdims=True))
    weights = jnp.where(allowed, jnp.exp(scores - row_max), 0.0)
    soft_weights = weights / lax.optimization_barrier(jnp.sum(weights, axis=-1, keepdims=True))
    probs_low = soft_weights.astype(bf16)
    out_slope = ((branch.astype(f32) - target.astype(f32)) * TOKENS ** (-0.5)).astype(bf16)
    grad_out = jnp.dot(attended.T, out_slope, preferred_element_type=f32)
    d_attended = jnp.dot(out_slope, w_out.T, preferred_element_type=f32).astype(bf16).reshape(row_count, KVH, group_size, HD)
    d_probs = jnp.einsum('qkgd,ckd->kgqc', d_attended.astype(f32), values_three.astype(f32))
    row_delta = lax.optimization_barrier(jnp.sum(soft_weights * d_probs, axis=-1, keepdims=True))
    d_scores = (soft_weights * (d_probs - row_delta) * scale).astype(bf16)
    dq_rot = jnp.einsum('kgqc,ckd->qkgd', d_scores.astype(f32), keys_three.astype(f32)).reshape(row_count, HEADS, HD)
    dk_rot = jnp.einsum('kgqc,qkgd->ckd', d_scores.astype(f32), grouped.astype(f32))
    dv_rows = jnp.einsum('kgqc,qkgd->ckd', probs_low.astype(f32), d_attended.astype(f32))
    d_query = unrotate(dq_rot, cos_table, sin_table).astype(bf16).reshape(row_count, HEADS * HD)
    d_key = unrotate(dk_rot, cos_table, sin_table).astype(bf16).reshape(row_count, KVH * HD)
    d_value = dv_rows.astype(bf16).reshape(row_count, KVH * HD)
    grad_query = jnp.dot(normed.T, d_query, preferred_element_type=f32)
    grad_key = jnp.dot(normed.T, d_key, preferred_element_type=f32)
    grad_value = jnp.dot(normed.T, d_value, preferred_element_type=f32)
    d_normed = jnp.dot(d_query, w_query.T, preferred_element_type=f32) + jnp.dot(d_key, w_key.T, preferred_element_type=f32) + jnp.dot(d_value, w_value.T, preferred_element_type=f32)
    grad_gain = lax.optimization_barrier(jnp.sum(d_normed * unit_rows, axis=0))
    scaled = d_normed * norm_gain[None, :]
    d_hidden = inv_rms * (scaled - unit_rows * lax.optimization_barrier(jnp.mean(scaled * unit_rows, axis=1, keepdims=True)))
    return (grad_query, grad_key, grad_value, grad_out, grad_gain, d_hidden)

def reference(hidden_in, teacher, row_source, segments, branch, queries, key_rot, value_rows, attended, norm_gain, w_query, w_key, w_value, w_out):
    target_all = jnp.take(teacher, row_source, axis=0)

    def one_group(totals, group_index):
        row_start = (group_index * TOK_GRP).astype(jnp.int32)

        def rows_of(array):
            return lax.dynamic_slice_in_dim(array, row_start, TOK_GRP, 0)
        segment_ids = lax.dynamic_index_in_dim(segments, group_index, 0, keepdims=False)
        grads = group_terms(rows_of(hidden_in), rows_of(target_all), rows_of(branch), rows_of(queries), rows_of(key_rot), rows_of(value_rows), rows_of(attended), segment_ids, norm_gain, w_query, w_key, w_value, w_out)
        updated = (totals[0] + rounded(grads[0]), totals[1] + rounded(grads[1]), totals[2] + rounded(grads[2]), totals[3] + rounded(grads[3]), totals[4] + grads[4])
        return (updated, grads[5])
    zeros = (jnp.zeros((D, HEADS * HD), jnp.float32), jnp.zeros((D, KVH * HD), jnp.float32), jnp.zeros((D, KVH * HD), jnp.float32), jnp.zeros((HEADS * HD, D), jnp.float32), jnp.zeros((D,), jnp.float32))
    totals, hidden_grads = lax.scan(one_group, zeros, jnp.arange(N_DP, dtype=jnp.int32))
    return (totals[0], totals[1], totals[2], totals[3], totals[4], hidden_grads.reshape(TOKENS, D))
```

```python
import functools

import jax
import jax.numpy as jnp
from jax import lax
from jax.experimental import pallas as pl
from jax.experimental.pallas import tpu as pltpu
from jax.sharding import PartitionSpec as P

HEADS = 32
KVH = 8
HD = 128
D = 4096
ROWS = 128
GROUP = 1024
N_DP = 16
N_TENSOR = 8
SLOTS = 16
PIECE = 32

MESH = pl.DeviceIdType.MESH
f32 = jnp.float32
bf16 = jnp.bfloat16
NT = (((1,), (1,)), ((), ()))

theta_base = 500000.0
eps_norm = 1e-05


def segment_positions(segment_ids):
    row_index = jnp.arange(segment_ids.shape[0], dtype=jnp.int32)
    before = jnp.sum((segment_ids[None, :] < segment_ids[:, None]).astype(jnp.int32), axis=1)
    return row_index - before


def place():
    d, t = lax.axis_index("dp"), lax.axis_index("tensor")
    return d, t, lax.div(t, 2), lax.rem(t, 2)


def tensor_index(x, z):
    return x * 2 + z


def greet(ids):
    barrier = pltpu.get_barrier_semaphore()
    for device in ids:
        pl.semaphore_signal(barrier, inc=1, device_id=device, device_id_type=MESH)
    pl.semaphore_wait(barrier, len(ids))


def remote(src, dst, send_sem, recv_sem, to):
    return pltpu.make_async_remote_copy(
        src_ref=src, dst_ref=dst, send_sem=send_sem, recv_sem=recv_sem, device_id=to, device_id_type=MESH
    )


class TreeGather:
    def __init__(self, own, full, send, recv):
        self.own, self.full, self.send_sems, self.recv_sems = own, full, send, recv
        self.d, self.t, self.x, self.z = place()
        self.copies = []
        d, x, z = self.d, self.x, self.z
        right, left, across, other = lax.rem(x + 1, 4), lax.rem(x + 3, 4), lax.rem(x + 2, 4), 1 - z
        self.to_right = (d, tensor_index(right, z))
        self.to_left = (d, tensor_index(left, z))
        self.to_z = (d, tensor_index(x, other))
        self.near = [tensor_index(x, other), tensor_index(left, z), tensor_index(right, z), tensor_index(across, z)]
        self.far = [tensor_index(left, other), tensor_index(right, other), tensor_index(across, other)]

    def piece(self, s, p):
        return self.full.at[pl.ds(pl.multiple_of(s * ROWS + p * PIECE, PIECE), PIECE)]

    def send(self, s, p, to, own=False):
        src = self.own.at[pl.ds(p * PIECE, PIECE)] if own else self.piece(s, p)
        copy = remote(src, self.piece(s, p), self.send_sems.at[len(self.copies)], self.recv_sems.at[s, p], to)
        copy.start()
        self.copies.append(copy)

    def wait(self, s, p):
        piece = self.piece(s, p)
        remote(piece, piece, self.send_sems.at[0], self.recv_sems.at[s, p], self.to_z).wait_recv()

    def begin(self):
        t = self.t
        for p, to in [
            (0, self.to_z), (2, self.to_right), (3, self.to_left), (1, self.to_z), (3, self.to_right), (2, self.to_left),
            (2, self.to_z), (0, self.to_right), (1, self.to_left), (3, self.to_z), (1, self.to_right), (0, self.to_left),
        ]:
            self.send(t, p, to, True)

    def steps(self):
        partner, left, right, across = self.near
        far_left, far_right, far_across = self.far
        to_z, to_left, to_right = self.to_z, self.to_left, self.to_right
        plan = [
            (partner, 0, (to_right, to_left)), (partner, 1, (to_left, to_right)),
            (left, 2, (to_right, to_z)), (right, 3, (to_left, to_z)), (left, 3, (to_z,)), (right, 2, (to_z,)),
            (left, 0, (to_right,)), (right, 1, (to_left,)), (across, 2, (to_z,)), (across, 3, (to_z,)),
            (far_left, 0, (to_right,)), (far_right, 1, (to_left,)),
            (left, 1, ()), (right, 0, ()), (across, 0, ()), (across, 1, ()),
            (far_left, 1, ()), (far_right, 0, ()), (far_across, 0, ()), (far_across, 1, ()),
        ] + [(s, p, ()) for s in (partner, far_left, far_right, far_across) for p in (2, 3)]

        def make(s, p, targets):
            def step():
                self.wait(s, p)
                for to in targets:
                    self.send(s, p, to)
            return step

        return [make(*entry) for entry in plan]

    def finish(self):
        for copy in self.copies:
            copy.wait_send()


def gather_kernel(
    source_ref, teacher_ref, branch_ref, hidden_ref,
    hidden_out, slope_out,
    sources, parcel, arrived, slope,
    source_send, source_recv, parcel_send, parcel_recv, hidden_send, hidden_recv, slope_send, slope_recv, local_sem,
):
    d, t, x, z = place()
    peers = [(lax.rem(d + k, N_DP), t) for k in range(1, N_DP)]
    hidden_tree = TreeGather(hidden_ref, hidden_out, hidden_send, hidden_recv)
    slope_tree = TreeGather(slope, slope_out, slope_send, slope_recv)
    greet(peers + [hidden_tree.to_right, hidden_tree.to_left, hidden_tree.to_z])

    source_copies = []
    for k, to in enumerate(peers):
        copy = remote(source_ref, sources.at[d], source_send.at[k], source_recv.at[k], to)
        copy.start()
        source_copies.append(copy)
    hidden_tree.begin()
    own_rows = pl.ds(pl.multiple_of(t * ROWS, ROWS), ROWS)
    keep_hidden = pltpu.make_async_copy(hidden_ref, hidden_out.at[own_rows], local_sem.at[0])
    keep_hidden.start()
    sources[d] = source_ref[...]

    above = (
        lax.broadcasted_iota(jnp.int32, (ROWS, ROWS), 0) < lax.broadcasted_iota(jnp.int32, (ROWS, ROWS), 1)
    ).astype(bf16)
    slot_ids = lax.broadcasted_iota(jnp.int32, (SLOTS, ROWS), 0)
    peer_ids = lax.broadcasted_iota(jnp.int32, (N_DP, ROWS), 0)
    row_ids = lax.broadcasted_iota(jnp.int32, (ROWS, ROWS), 0)

    def slot_onehot(mask, rank, q):
        return ((slot_ids == rank[q:q + 1]) & (mask[q:q + 1] > 0)).astype(f32).astype(bf16)

    def ranks(mask):
        return jnp.dot(mask.astype(bf16), above, preferred_element_type=f32).astype(jnp.int32)

    own_source = source_ref[0:1, :]
    from_peer = (peer_ids == lax.shift_right_logical(own_source, 10)).astype(f32)
    from_rank = ranks(from_peer)
    place_rows = jnp.concatenate([slot_onehot(from_peer, from_rank, q) for q in range(N_DP)], axis=0)
    place_rows = place_rows.astype(f32).T.astype(bf16)

    for copy in source_copies:
        copy.wait_recv()
    wanted = jnp.concatenate([sources[q, 0:1, :] for q in range(N_DP)], axis=0)
    mine = (lax.shift_right_logical(wanted, 10) == d).astype(f32)
    rank = ranks(mine)
    local_row = jnp.bitwise_and(wanted, ROWS - 1)
    picks = []
    for q in range(N_DP):
        row_onehot = (row_ids == local_row[q:q + 1]).astype(f32).astype(bf16)
        picks.append(lax.dot_general(slot_onehot(mine, rank, q), row_onehot, NT, preferred_element_type=f32))
    pick = jnp.concatenate(picks, axis=0).astype(bf16)
    for n in range(0, D, 512):
        parcel[:, n:n + 512] = jnp.dot(pick, teacher_ref[:, n:n + 512], preferred_element_type=f32).astype(bf16)

    own_slots = pl.ds(pl.multiple_of(d * SLOTS, SLOTS), SLOTS)
    parcel_copies = []
    for k, to in enumerate(peers):
        slots = pl.ds(pl.multiple_of(to[0] * SLOTS, SLOTS), SLOTS)
        copy = remote(parcel.at[slots], arrived.at[own_slots], parcel_send.at[k], parcel_recv.at[k], to)
        copy.start()
        parcel_copies.append(copy)
    arrived[own_slots, :] = parcel[own_slots, :]

    hidden_steps = hidden_tree.steps()
    for step in hidden_steps[:10]:
        step()
    for copy in parcel_copies:
        copy.wait_recv()
    for n in range(0, D, 512):
        target = jnp.dot(place_rows, arrived[:, n:n + 512], preferred_element_type=f32)
        slope[:, n:n + 512] = ((branch_ref[:, n:n + 512].astype(f32) - target) * (N_DP * GROUP) ** -0.5).astype(bf16)
    slope_tree.begin()
    keep_slope = pltpu.make_async_copy(slope, slope_out.at[own_rows], local_sem.at[1])
    keep_slope.start()
    for step in hidden_steps[10:]:
        step()
    for step in slope_tree.steps():
        step()
    hidden_tree.finish()
    slope_tree.finish()
    for copy in source_copies + parcel_copies:
        copy.wait_send()
    keep_hidden.wait()
    keep_slope.wait()


def gather_call(row_source, teacher, branch, hidden_in):
    any_space = pl.BlockSpec(memory_space=pl.ANY)
    vmem = pl.BlockSpec(memory_space=pltpu.VMEM)
    dma = pltpu.SemaphoreType.DMA
    return pl.pallas_call(
        gather_kernel,
        out_shape=(jax.ShapeDtypeStruct((GROUP, D), bf16), jax.ShapeDtypeStruct((GROUP, D), bf16)),
        in_specs=[vmem, vmem, vmem, any_space],
        out_specs=(any_space, any_space),
        scratch_shapes=[
            pltpu.VMEM((N_DP, 8, ROWS), jnp.int32),
            pltpu.VMEM((N_DP * SLOTS, D), bf16),
            pltpu.VMEM((N_DP * SLOTS, D), bf16),
            pltpu.VMEM((ROWS, D), bf16),
            dma((15,)), dma((15,)), dma((15,)), dma((15,)),
            dma((28,)), dma((8, 4)), dma((28,)), dma((8, 4)), dma((2,)),
        ],
        compiler_params=pltpu.CompilerParams(
            collective_id=1, has_side_effects=True, vmem_limit_bytes=48 * 2**20
        ),
        cost_estimate=pl.CostEstimate(flops=10**9, bytes_accessed=24 * 2**20, transcendentals=0),
    )(jnp.broadcast_to(row_source[None, :], (8, ROWS)), teacher, branch, hidden_in)


def attention_kernel(
    q_ref, k_ref, v_ref, da_ref, seg_row_ref, seg_col_ref, cos_ref, sin_ref,
    dqkv_ref, dqkv_t_ref, dk_acc, dv_acc,
):
    blk = 256
    scale = HD ** -0.5
    dk_acc[...] = jnp.zeros_like(dk_acc)
    dv_acc[...] = jnp.zeros_like(dv_acc)
    k_t = k_ref[...].astype(f32).T.astype(bf16)

    def rotate_back(values, columns):
        u, w = values[:64], values[64:]
        c, s = cos_ref[:, columns], sin_ref[:, columns]
        return jnp.concatenate([u * c + w * s, w * c - u * s], axis=0)

    for i in range(GROUP // blk):
        rows = slice(i * blk, (i + 1) * blk)
        seen = (i + 1) * blk
        allowed = (seg_col_ref[:seen, :] == seg_row_ref[:, rows]) & (
            lax.broadcasted_iota(jnp.int32, (seen, blk), 0) <= lax.broadcasted_iota(jnp.int32, (seen, blk), 1) + i * blk
        )
        for h in range(4):
            cols = slice(h * HD, (h + 1) * HD)
            q = q_ref[rows, cols]
            da = da_ref[rows, cols]
            scores = lax.dot_general(k_ref[:seen, :], q, NT, preferred_element_type=f32) * scale
            scores = jnp.where(allowed, scores, -1e30)
            weights = jnp.where(allowed, jnp.exp(scores - jnp.max(scores, axis=0, keepdims=True)), 0.0)
            soft = weights * (1.0 / jnp.sum(weights, axis=0, keepdims=True))
            d_probs = lax.dot_general(v_ref[:seen, :], da, NT, preferred_element_type=f32)
            delta = jnp.sum(soft * d_probs, axis=0, keepdims=True)
            d_scores = (soft * (d_probs - delta) * scale).astype(bf16)
            dv_acc[:seen, :] += jnp.dot(soft.astype(bf16), da, preferred_element_type=f32)
            dk_acc[:seen, :] += jnp.dot(d_scores, q, preferred_element_type=f32)
            dq_t = jnp.dot(k_t[:, :seen], d_scores, preferred_element_type=f32)
            dq_t = rotate_back(dq_t, rows)
            dqkv_t_ref[cols, rows] = dq_t.astype(bf16)
            dqkv_ref[rows, cols] = dq_t.T.astype(bf16)
    dk_t = rotate_back(dk_acc[...].T, slice(0, GROUP))
    dqkv_t_ref[512:640, :] = dk_t.astype(bf16)
    dqkv_ref[:, 512:640] = dk_t.T.astype(bf16)
    dqkv_t_ref[640:768, :] = dv_acc[...].T.astype(bf16)
    dqkv_ref[:, 640:768] = dv_acc[...].astype(bf16)


def attention_call(queries, key_rot, value_rows, d_attended, segment_ids):
    positions = segment_positions(segment_ids)
    frequency = theta_base ** (-2.0 * jnp.arange(HD // 2, dtype=f32) / HD)
    angles = frequency[:, None] * positions.astype(f32)[None, :]
    vmem = pl.BlockSpec(memory_space=pltpu.VMEM)
    return pl.pallas_call(
        attention_kernel,
        out_shape=(jax.ShapeDtypeStruct((GROUP, 768), bf16), jax.ShapeDtypeStruct((768, GROUP), bf16)),
        in_specs=[vmem] * 8,
        out_specs=(vmem, vmem),
        scratch_shapes=[pltpu.VMEM((GROUP, HD), f32), pltpu.VMEM((GROUP, HD), f32)],
        compiler_params=pltpu.CompilerParams(vmem_limit_bytes=48 * 2**20),
        cost_estimate=pl.CostEstimate(flops=6 * 10**9, bytes_accessed=8 * 2**20, transcendentals=4 * 2**20),
    )(
        queries, key_rot, value_rows, d_attended, segment_ids[None, :], segment_ids[:, None],
        jnp.cos(angles), jnp.sin(angles),
    )


class TreeScatter:
    def __init__(self, part, slots, send, recv):
        self.part, self.slots, self.send_sems, self.recv_sems = part, slots, send, recv
        self.d, self.t, self.x, self.z = place()
        d, x, z = self.d, self.x, self.z
        self.to_right = (d, tensor_index(lax.rem(x + 1, 4), z))
        self.to_left = (d, tensor_index(lax.rem(x + 3, 4), z))
        self.to_z = (d, tensor_index(x, 1 - z))
        names = [(kind, e, p) for e in (0, 1) for p in (0, 1) for kind in ("relay", "right", "left")]
        names += [("z", 0, p) for p in (0, 1)]
        names += [("zz", k, p) for k in range(4) for p in (2, 3)]
        names += [(kind, 0, p) for p in (2, 3) for kind in ("relay", "right", "left")]
        self.index = {name: n for n, name in enumerate(names)}
        self.copies = []

    def dest(self, k, e):
        z = self.z if e == 0 else 1 - self.z
        return tensor_index(lax.rem(self.x + k, 4), z)

    def rows(self, p):
        return pl.ds(p * PIECE, PIECE)

    def send(self, k, e, p, to, name):
        n = self.index[name]
        copy = remote(
            self.part.at[self.dest(k, e), self.rows(p)], self.slots.at[n], self.send_sems.at[len(self.copies)],
            self.recv_sems.at[n], to,
        )
        copy.start()
        self.copies.append(copy)

    def wait(self, name):
        n = self.index[name]
        slot = self.slots.at[n]
        remote(slot, slot, self.send_sems.at[0], self.recv_sems.at[n], self.to_z).wait_recv()

    def add(self, k, e, p, names):
        for name in names:
            self.wait(name)
        s = self.dest(k, e)
        for n in range(0, D, 512):
            columns = slice(n, n + 512)
            total = self.part[s, self.rows(p), columns].astype(f32)
            for name in names:
                total = total + self.slots[self.index[name], :, columns].astype(f32)
            self.part[s, self.rows(p), columns] = total.astype(bf16)

    def begin_z(self):
        for k in (2, 1, 3, 0):
            for p in (2, 3):
                self.send(k, 1, p, self.to_z, ("zz", k, p))

    def begin_x(self, e, p):
        if p % 2 == 0:
            self.send(2, e, p, self.to_left, ("relay", e, p))
            self.send(1, e, p, self.to_right, ("left", e, p))
        else:
            self.send(2, e, p, self.to_right, ("relay", e, p))
            self.send(3, e, p, self.to_left, ("right", e, p))

    def relay(self, e, p):
        if p % 2 == 0:
            self.add(3, e, p, [("relay", e, p)])
            self.send(3, e, p, self.to_left, ("right", e, p))
        else:
            self.add(1, e, p, [("relay", e, p)])
            self.send(1, e, p, self.to_right, ("left", e, p))

    def z_done(self, k, p):
        self.add(k, 0, p, [("zz", k, p)])

    def root_other(self, p):
        self.add(0, 1, p, [("right", 1, p), ("left", 1, p)])
        self.send(0, 1, p, self.to_z, ("z", 0, p))

    def root_names(self, p):
        names = [("right", 0, p), ("left", 0, p)]
        return names + [("z", 0, p)] if p < 2 else names

    def finish(self):
        for copy in self.copies:
            copy.wait_send()


class StageScatter:
    def __init__(self, part, core, ring, half, sems):
        self.part, self.core, self.ring, self.half = part, core, ring, half
        self.core_send, self.core_recv, self.ring_send, self.ring_recv, self.half_send, self.half_recv = sems
        d, t, _, _ = place()
        self.c, self.y, self.zh = lax.rem(d, 2), lax.rem(lax.div(d, 2), 4), lax.div(d, 8)
        self.to_core = (d + 1 - 2 * self.c, t)
        self.to_ring = [((self.zh * 4 + lax.rem(self.y + k, 4)) * 2 + self.c, t) for k in (1, 2, 3)]
        self.to_half = (((1 - self.zh) * 4 + self.y) * 2 + self.c, t)
        self.late = []

    def core_copy(self, j):
        return remote(self.part.at[1 - self.c, j], self.core.at[j], self.core_send.at[j], self.core_recv.at[j], self.to_core)

    def fold_core(self, j):
        self.core_copy(j).wait_recv()
        self.part[self.c, j] = (self.part[self.c, j].astype(f32) + self.core[j].astype(f32)).astype(bf16)

    def fold_and_send_ring(self):
        for k in (2, 1, 3):
            y = lax.rem(self.y + k, 4)
            for half in (0, 1):
                zh = 1 - self.zh if half == 0 else self.zh
                j = zh * 4 + y
                self.fold_core(j)
                copy = remote(
                    self.part.at[self.c, j], self.ring.at[k - 1, half], self.ring_send.at[k - 1, half],
                    self.ring_recv.at[k - 1, half], self.to_ring[k - 1],
                )
                copy.start()
                self.late.append(copy)
        for half in (0, 1):
            self.fold_core((1 - self.zh if half == 0 else self.zh) * 4 + self.y)

    def ring_total(self, half):
        for k in range(3):
            remote(
                self.ring.at[k, half], self.ring.at[k, half], self.ring_send.at[k, half], self.ring_recv.at[k, half],
                self.to_core,
            ).wait_recv()
        j = (1 - self.zh if half == 0 else self.zh) * 4 + self.y
        total = self.part[self.c, j].astype(f32)
        for k in range(3):
            total = total + self.ring[k, half].astype(f32)
        return j, total

    def send_half(self):
        j, total = self.ring_total(0)
        self.part[self.c, j] = total.astype(bf16)
        copy = remote(self.part.at[self.c, j], self.half, self.half_send, self.half_recv, self.to_half)
        copy.start()
        self.late.append(copy)

    def result(self):
        _, total = self.ring_total(1)
        self.late[-1].wait_recv()
        return total + self.half[...].astype(f32)

    def finish(self):
        for copy in self.late:
            copy.wait_send()
        for j in range(8):
            self.core_copy(j).wait_send()


def scatter_kernel(
    dqkv_ref, dqkv_t_ref, wq_ref, wk_ref, wv_ref, hidden_ref, inv_ref, gain_ref, out_part_ref,
    dh_ref, gqkv_ref, gout_ref, ggain_ref,
    part, slots, qkv_part, qkv_core, qkv_ring, qkv_half, out_part, out_core, out_ring, out_half,
    gain_sum, gain_block, gain_tensor, gain_dp,
    part_send, part_recv,
    qkv_core_send, qkv_core_recv, qkv_ring_send, qkv_ring_recv, qkv_half_send, qkv_half_recv,
    out_core_send, out_core_recv, out_ring_send, out_ring_recv, out_half_send, out_half_recv,
    gain_t_send, gain_t_recv, gain_d_send, gain_d_recv, local_sem,
):
    d, t, x, z = place()
    tree = TreeScatter(part, slots, part_send, part_recv)
    qkv = StageScatter(
        qkv_part, qkv_core, qkv_ring, qkv_half,
        (qkv_core_send, qkv_core_recv, qkv_ring_send, qkv_ring_recv, qkv_half_send.at[0], qkv_half_recv.at[0]),
    )
    out = StageScatter(
        out_part, out_core, out_ring, out_half,
        (out_core_send, out_core_recv, out_ring_send, out_ring_recv, out_half_send.at[0], out_half_recv.at[0]),
    )
    tensor_peers = [(d, lax.rem(t + k, N_TENSOR)) for k in range(1, N_TENSOR)]
    dp_peers = [(lax.rem(d + k, N_DP), t) for k in range(1, N_DP)]
    load = pltpu.make_async_copy(out_part_ref, out_part, local_sem.at[0])
    load.start()
    greet(tensor_peers + dp_peers)
    load.wait()

    for j in range(8):
        out.core_copy(j).start()

    gain_sum[...] = jnp.zeros_like(gain_sum)

    def partials(first):
        rows = slice(first, first + 64)

        def tile(n, carry):
            columns = pl.ds(pl.multiple_of(n * 256, 256), 256)
            lhs = dqkv_ref[:, rows, :].reshape(512, 768)
            total = lax.dot_general(lhs[:, :512], wq_ref[columns, :], NT, preferred_element_type=f32)
            total += lax.dot_general(lhs[:, 512:640], wk_ref[columns, :], NT, preferred_element_type=f32)
            total += lax.dot_general(lhs[:, 640:768], wv_ref[columns, :], NT, preferred_element_type=f32)
            part[:, rows, columns] = total.astype(bf16).reshape(8, 64, 256)
            unit = hidden_ref[:, rows, columns].astype(f32) * inv_ref[:, rows, :]
            gain_sum[:, columns] += jnp.sum((total * unit.reshape(512, 256)).reshape(64, 8, 256), axis=0)
            return carry

        lax.fori_loop(0, D // 256, tile, 0)

    partials(64)
    tree.begin_z()
    partials(0)
    for e in (1, 0):
        for p in (0, 1):
            tree.begin_x(e, p)

    gain_row = jnp.sum(gain_sum[...], axis=0, keepdims=True)
    for i in range(32):
        gain_block[0, i:i + 1, :] = gain_row[:, i * 128:(i + 1) * 128]
    gain_tensor[t] = gain_block[0]
    gain_copies = []
    for k, to in enumerate(tensor_peers):
        copy = remote(gain_block.at[0], gain_tensor.at[t], gain_t_send.at[k], gain_t_recv.at[k], to)
        copy.start()
        gain_copies.append(copy)

    def projection(core):
        def tile(j, carry):
            columns = pl.ds(pl.multiple_of((2 * j + core) * 256, 256), 256)
            normed = (
                (hidden_ref[:, :, columns].astype(f32) * inv_ref[...]) * gain_ref[:, columns].reshape(1, 1, 256)
            ).astype(bf16).reshape(GROUP, 256)
            qkv_part[core, j] = jnp.dot(dqkv_t_ref[...], normed, preferred_element_type=f32).astype(bf16)
            return carry

        lax.fori_loop(0, 8, tile, 0)

    projection(1 - qkv.c)
    for j in range(8):
        qkv.core_copy(j).start()
    out.fold_and_send_ring()
    projection(qkv.c)
    for e in (1, 0):
        for p in (0, 1):
            tree.relay(e, p)
    qkv.fold_and_send_ring()

    for copy in gain_copies:
        copy.wait_recv()
    gain_total = gain_tensor[0]
    for k in range(1, N_TENSOR):
        gain_total = gain_total + gain_tensor[k]
    gain_block[1] = gain_total
    gain_dp[d] = gain_total
    dp_copies = []
    for k, to in enumerate(dp_peers):
        copy = remote(gain_block.at[1], gain_dp.at[d], gain_d_send.at[k], gain_d_recv.at[k], to)
        copy.start()
        dp_copies.append(copy)

    for p in (2, 3):
        tree.z_done(2, p)
        tree.z_done(1 if p == 2 else 3, p)
        tree.begin_x(0, p)
    for p in (0, 1):
        tree.root_other(p)
    for p in (2, 3):
        tree.z_done(3 if p == 2 else 1, p)
        tree.relay(0, p)
        tree.z_done(0, p)
    out.send_half()
    qkv.send_half()
    gout_ref[...] = out.result()

    for copy in dp_copies:
        copy.wait_recv()
    gain_total = gain_dp[0]
    for k in range(1, N_DP):
        gain_total = gain_total + gain_dp[k]
    ggain_ref[...] = gain_total

    for p in (0, 1, 2, 3):
        names = tree.root_names(p)
        for name in names:
            tree.wait(name)
        rows = slice(p * PIECE, (p + 1) * PIECE)
        total = part[t, rows, :].astype(f32)
        for name in names:
            total = total + slots[tree.index[name]].astype(f32)
        inv = inv_ref[t, rows, :]
        unit = hidden_ref[t, rows, :].astype(f32) * inv
        scaled = total * gain_ref[...]
        mean = jnp.sum(scaled * unit, axis=1, keepdims=True) * (1.0 / D)
        dh_ref[rows, :] = inv * (scaled - unit * mean)
    gqkv_ref[...] = qkv.result()

    tree.finish()
    out.finish()
    qkv.finish()
    for copy in gain_copies + dp_copies:
        copy.wait_send()


def scatter_call(dqkv, dqkv_t, w_query, w_key, w_value, hidden, inv_rms, gain, out_part):
    any_space = pl.BlockSpec(memory_space=pl.ANY)
    vmem = pl.BlockSpec(memory_space=pltpu.VMEM)
    dma = pltpu.SemaphoreType.DMA
    stage_sems = [dma((8,)), dma((8,)), dma((3, 2)), dma((3, 2)), dma((1,)), dma((1,))]
    return pl.pallas_call(
        scatter_kernel,
        out_shape=(
            jax.ShapeDtypeStruct((ROWS, D), f32), jax.ShapeDtypeStruct((768, 256), f32),
            jax.ShapeDtypeStruct((512, 256), f32), jax.ShapeDtypeStruct((32, 128), f32),
        ),
        in_specs=[vmem] * 8 + [any_space],
        out_specs=(vmem,) * 4,
        scratch_shapes=[
            pltpu.VMEM((8, ROWS, D), bf16), pltpu.VMEM((28, PIECE, D), bf16),
            pltpu.VMEM((2, 8, 768, 256), bf16), pltpu.VMEM((8, 768, 256), bf16),
            pltpu.VMEM((3, 2, 768, 256), bf16), pltpu.VMEM((768, 256), bf16),
            pltpu.VMEM((2, 8, 512, 256), bf16), pltpu.VMEM((8, 512, 256), bf16),
            pltpu.VMEM((3, 2, 512, 256), bf16), pltpu.VMEM((512, 256), bf16),
            pltpu.VMEM((8, D), f32), pltpu.VMEM((2, 32, 128), f32),
            pltpu.VMEM((N_TENSOR, 32, 128), f32), pltpu.VMEM((N_DP, 32, 128), f32),
            dma((28,)), dma((28,)),
        ] + stage_sems + stage_sems + [dma((7,)), dma((7,)), dma((15,)), dma((15,)), dma((1,))],
        compiler_params=pltpu.CompilerParams(
            collective_id=2, has_side_effects=True, vmem_limit_bytes=62 * 2**20
        ),
        cost_estimate=pl.CostEstimate(flops=14 * 10**9, bytes_accessed=40 * 2**20, transcendentals=0),
    )(
        dqkv.reshape(8, ROWS, 768), dqkv_t, w_query, w_key, w_value, hidden.reshape(8, ROWS, D),
        inv_rms.reshape(8, ROWS, 1), gain, out_part,
    )


def per_device(
    hidden_in, teacher, row_source, segments, branch, queries, key_rot, value_rows, attended, norm_gain,
    w_query, w_key, w_value, w_out,
):
    hidden, slope = gather_call(row_source, teacher, branch, hidden_in)
    floated = hidden.astype(f32)
    inv_rms = lax.rsqrt(jnp.mean(floated * floated, axis=1, keepdims=True) + eps_norm)
    grad_out = lax.dot_general(attended, slope, (((0,), (0,)), ((), ())), preferred_element_type=f32)
    out_part = jnp.transpose(grad_out.astype(bf16).reshape(512, 8, 2, 256), (2, 1, 0, 3))
    d_attended = lax.dot_general(slope, w_out, NT, preferred_element_type=f32).astype(bf16)
    dqkv, dqkv_t = attention_call(queries, key_rot, value_rows, d_attended, segments[0])
    d_hidden, grad_qkv, grad_out, grad_gain = scatter_call(
        dqkv, dqkv_t, w_query, w_key, w_value, hidden, inv_rms, norm_gain[None, :], out_part
    )
    grads = grad_qkv.T
    return (grads[:, :512], grads[:, 512:640], grads[:, 640:768], grad_out, grad_gain.reshape(D), d_hidden)


def solution(mesh):
    return jax.shard_map(
        per_device,
        mesh=mesh,
        in_specs=(
            P(("dp", "tensor"), None),
            P(("dp", "tensor"), None),
            P(("dp", "tensor")),
            P("dp", None),
            P(("dp", "tensor"), None),
            P("dp", "tensor"),
            P("dp", "tensor"),
            P("dp", "tensor"),
            P("dp", "tensor"),
            P(),
            P(None, "tensor"),
            P(None, "tensor"),
            P(None, "tensor"),
            P("tensor", None),
        ),
        out_specs=(
            P("dp", "tensor"),
            P("dp", "tensor"),
            P("dp", "tensor"),
            P("tensor", "dp"),
            P(),
            P(("dp", "tensor"), None),
        ),
        check_vma=False,
    )
```

```python
import jax
import jax.numpy as jnp
import numpy as np
from jax import lax
from jax.experimental import pallas as pl
from jax.experimental.pallas import tpu as pltpu
from jax.sharding import PartitionSpec as P

HEADS = 32
KVH = 8
HD = 128
D = 4096
ROWS = 128
GROUP = 1024
N_DP = 16
N_TENSOR = 8
SLOTS = 16
PIECE = 32
STRIPE = 1024
TILE = 256

MESH = pl.DeviceIdType.MESH
f32 = jnp.float32
bf16 = jnp.bfloat16
NT = (((1,), (1,)), ((), ()))

theta_base = 500000.0
eps_norm = 1e-05


def place():
    d, t = lax.axis_index("dp"), lax.axis_index("tensor")
    return d, t, lax.div(t, 2), lax.rem(t, 2)


def tensor_index(x, z):
    return x * 2 + z


def greet(ids):
    barrier = pltpu.get_barrier_semaphore()
    for device in ids:
        pl.semaphore_signal(barrier, inc=1, device_id=device, device_id_type=MESH)
    pl.semaphore_wait(barrier, len(ids))


def remote(src, dst, send_sem, recv_sem, to):
    return pltpu.make_async_remote_copy(
        src_ref=src, dst_ref=dst, send_sem=send_sem, recv_sem=recv_sem, device_id=to, device_id_type=MESH
    )


class TreeGather:
    def __init__(self, own, full, send, recv, over_z):
        self.over_z = over_z
        self.own, self.full, self.send_sems, self.recv_sems = own, full, send, recv
        self.d, self.t, self.x, self.z = place()
        self.copies = []
        d, x, z = self.d, self.x, self.z
        right, left, across, other = lax.rem(x + 1, 4), lax.rem(x + 3, 4), lax.rem(x + 2, 4), 1 - z
        self.to_right = (d, tensor_index(right, z))
        self.to_left = (d, tensor_index(left, z))
        self.to_z = (d, tensor_index(x, other))
        self.near = [tensor_index(x, other), tensor_index(left, z), tensor_index(right, z), tensor_index(across, z)]
        self.far = [tensor_index(left, other), tensor_index(right, other), tensor_index(across, other)]

    def piece(self, s, p):
        return self.full.at[s, pl.ds(p * PIECE, PIECE)]

    def send(self, s, p, to, own=False):
        src = self.own.at[pl.ds(p * PIECE, PIECE)] if own else self.piece(s, p)
        copy = remote(src, self.piece(s, p), self.send_sems.at[len(self.copies)], self.recv_sems.at[s, p], to)
        copy.start()
        self.copies.append(copy)

    def wait(self, s, p):
        piece = self.piece(s, p)
        remote(piece, piece, self.send_sems.at[0], self.recv_sems.at[s, p], self.to_z).wait_recv()

    def begin(self):
        by_z = list(range(4))
        by_x = list(range(self.over_z, 4)) + list(range(self.over_z))
        for i in (0, 2):
            a, b = by_x[i:i + 2]
            for p, to in (
                (by_z[i], self.to_z), (a, self.to_right), (b, self.to_left), (by_z[i + 1], self.to_z),
                (b, self.to_right), (a, self.to_left),
            ):
                if to is not self.to_z or p < self.over_z or self.over_z < 4:
                    self.send(self.t, p, to, self.own is not None)

    def steps(self):
        partner, left, right, across = self.near
        far_left, far_right, far_across = self.far
        first = list(range(self.over_z))
        last = list(range(self.over_z, 4))
        order = [(partner, p) for p in first[:2]] + [(s, p) for p in (last + first)[:2] for s in (left, right)]
        order += [(partner, p) for p in first[2:]] + [(s, p) for p in (last + first)[2:] for s in (left, right)]
        order += [(s, p) for p in first for s in (far_left, far_right)] + [(across, p) for p in last + first]
        order += [(far_across, p) for p in first]
        order += [(s, p) for s in (partner, far_left, far_right, far_across) for p in last]

        def targets_of(s, p):
            targets = []
            if s is partner and p < self.over_z:
                targets += [self.to_right, self.to_left]
            if s is left and p % 2 == 0 or s is far_left and p % 2 == 0 and p < self.over_z:
                targets.append(self.to_right)
            if s is right and p % 2 == 1 or s is far_right and p % 2 == 1 and p < self.over_z:
                targets.append(self.to_left)
            if p >= self.over_z and (s is left or s is right or s is across):
                targets.append(self.to_z)
            return targets

        plan = [(s, p, targets_of(s, p)) for s, p in order]

        def make(s, p, targets):
            def step():
                self.wait(s, p)
                for to in targets:
                    self.send(s, p, to)
            return step

        return [make(*entry) for entry in plan]

    def finish(self):
        for copy in self.copies:
            copy.wait_send()


class TreeScatter:
    def __init__(self, part, slots, send, recv, over_z):
        self.over_z = over_z
        first, last = range(over_z), range(over_z, 4)
        self.part, self.slots, self.send_sems, self.recv_sems = part, slots, send, recv
        self.d, self.t, self.x, self.z = place()
        d, x, z = self.d, self.x, self.z
        self.to_right = (d, tensor_index(lax.rem(x + 1, 4), z))
        self.to_left = (d, tensor_index(lax.rem(x + 3, 4), z))
        self.to_z = (d, tensor_index(x, 1 - z))
        names = [(kind, e, p) for e in (0, 1) for p in first for kind in ("relay", "right", "left")]
        names += [("z", 0, p) for p in first]
        names += [("zz", k, p) for k in range(4) for p in last]
        names += [(kind, 0, p) for p in last for kind in ("relay", "right", "left")]
        self.index = {name: n for n, name in enumerate(names)}
        self.copies = []

    def dest(self, k, e):
        z = self.z if e == 0 else 1 - self.z
        return tensor_index(lax.rem(self.x + k, 4), z)

    def stripe(self, p):
        return pl.ds(p * STRIPE, STRIPE)

    def send(self, k, e, p, to, name):
        n = self.index[name]
        copy = remote(
            self.part.at[self.dest(k, e), :, self.stripe(p)], self.slots.at[n], self.send_sems.at[len(self.copies)],
            self.recv_sems.at[n], to,
        )
        copy.start()
        self.copies.append(copy)

    def wait(self, name):
        n = self.index[name]
        slot = self.slots.at[n]
        remote(slot, slot, self.send_sems.at[0], self.recv_sems.at[n], self.to_z).wait_recv()

    def total(self, k, e, p, names):
        for name in names:
            self.wait(name)
        total = self.part[self.dest(k, e), :, self.stripe(p)].astype(f32)
        for name in names:
            total = total + self.slots[self.index[name]].astype(f32)
        return total

    def add(self, k, e, p, names):
        self.part[self.dest(k, e), :, self.stripe(p)] = self.total(k, e, p, names).astype(bf16)

    def begin_z(self, p):
        for k in (2, 1, 3, 0):
            self.send(k, 1, p, self.to_z, ("zz", k, p))

    def begin_x(self, e, p):
        if p % 2 == 0:
            self.send(2, e, p, self.to_left, ("relay", e, p))
            self.send(1, e, p, self.to_right, ("left", e, p))
        else:
            self.send(2, e, p, self.to_right, ("relay", e, p))
            self.send(3, e, p, self.to_left, ("right", e, p))

    def relay(self, e, p):
        if p % 2 == 0:
            self.add(3, e, p, [("relay", e, p)])
            self.send(3, e, p, self.to_left, ("right", e, p))
        else:
            self.add(1, e, p, [("relay", e, p)])
            self.send(1, e, p, self.to_right, ("left", e, p))

    def z_done(self, k, p):
        self.add(k, 0, p, [("zz", k, p)])

    def root_other(self, p):
        self.add(0, 1, p, [("right", 1, p), ("left", 1, p)])
        self.send(0, 1, p, self.to_z, ("z", 0, p))

    def result(self, p):
        names = [("right", 0, p), ("left", 0, p)]
        return self.total(0, 0, p, names + [("z", 0, p)] if p < self.over_z else names)

    def finish(self):
        for copy in self.copies:
            copy.wait_send()


class StageScatter:
    def __init__(self, part, core, ring, half, sems):
        self.part, self.core, self.ring, self.half = part, core, ring, half
        self.core_send, self.core_recv, self.ring_send, self.ring_recv, self.half_send, self.half_recv = sems
        d, t, _, _ = place()
        self.c, self.y, self.zh = lax.rem(d, 2), lax.rem(lax.div(d, 2), 4), lax.div(d, 8)
        self.to_core = (d + 1 - 2 * self.c, t)
        self.to_right = ((self.zh * 4 + lax.rem(self.y + 1, 4)) * 2 + self.c, t)
        self.to_left = ((self.zh * 4 + lax.rem(self.y + 3, 4)) * 2 + self.c, t)
        self.to_half = (((1 - self.zh) * 4 + self.y) * 2 + self.c, t)
        self.cut = core.shape[1] // 2
        self.copies = []

    def core_copy(self, j):
        return remote(
            self.part.at[2 * j + 1 - self.c], self.core.at[j], self.core_send.at[j], self.core_recv.at[j], self.to_core
        )

    def block(self, k, half):
        zh = 1 - self.zh if half == 0 else self.zh
        return 2 * (zh * 4 + lax.rem(self.y + k, 4)) + self.c

    def fold_core(self, k, half):
        n = self.block(k, half)
        j = lax.div(n, 2)
        self.core_copy(j).wait_recv()
        self.part[n] = (self.part[n].astype(f32) + self.core[j].astype(f32)).astype(bf16)

    def rows(self, b):
        return pl.ds(b * self.cut, self.cut)

    def send(self, k, half, b, to, slot):
        copy = remote(
            self.part.at[self.block(k, half), self.rows(b)], self.ring.at[half, slot],
            self.ring_send.at[half, slot], self.ring_recv.at[half, slot], to,
        )
        copy.start()
        self.copies.append(copy)

    def wait(self, half, slot):
        ref = self.ring.at[half, slot]
        remote(ref, ref, self.ring_send.at[half, slot], self.ring_recv.at[half, slot], self.to_core).wait_recv()

    def begin_ring(self, half):
        self.fold_core(2, half)
        self.send(2, half, 0, self.to_left, 0)
        self.send(2, half, 1, self.to_right, 1)
        self.fold_core(1, half)
        self.send(1, half, 0, self.to_right, 2)
        self.fold_core(3, half)
        self.send(3, half, 1, self.to_left, 5)
        self.fold_core(0, half)

    def relay_ring(self, half):
        for k, b, slot, to, target in ((3, 0, 0, self.to_left, 4), (1, 1, 1, self.to_right, 3)):
            self.wait(half, slot)
            n = self.block(k, half)
            total = self.part[n, self.rows(b)].astype(f32) + self.ring[half, slot].astype(f32)
            self.part[n, self.rows(b)] = total.astype(bf16)
            self.send(k, half, b, to, target)

    def ring_total(self, half, b):
        total = self.part[self.block(0, half), self.rows(b)].astype(f32)
        for slot in (2 + b, 4 + b):
            self.wait(half, slot)
            total = total + self.ring[half, slot].astype(f32)
        return total

    def send_half(self):
        n = self.block(0, 0)
        for b in (0, 1):
            self.part[n, self.rows(b)] = self.ring_total(0, b).astype(bf16)
        copy = remote(self.part.at[n], self.half, self.half_send, self.half_recv, self.to_half)
        copy.start()
        self.half_copy = copy

    def result(self):
        totals = [self.ring_total(1, b) for b in (0, 1)]
        self.half_copy.wait_recv()
        return [total + self.half[self.rows(b), :].astype(f32) for b, total in enumerate(totals)]

    def finish(self):
        for copy in self.copies:
            copy.wait_send()
        self.half_copy.wait_send()
        for j in range(8):
            self.core_copy(j).wait_send()


def kernel(
    source_ref, seg_ref, freq_ref, gain_ref, teacher_ref, branch_ref, hidden_ref, q_in, k_in, v_in, att_in, wq_in, wk_in,
    wv_in, w_out_in,
    dh_ref, gq_ref, gk_ref, gv_ref, gout_ref, ggain_ref, hidden_full,
    part, slope, slots, qkv_part, qkv_core, qkv_ring, qkv_half, out_part, out_core, out_ring, out_half,
    att_t, d_att, q_ref, k_ref, v_ref, cos_ref, sin_ref, seg_col, inv_own, inv_all, dk_acc, dv_acc,
    request, sources, gain_sum, gain_block, gain_tensor, gain_dp,
    source_send, source_recv, parcel_send, parcel_recv, hidden_send, hidden_recv, slope_send, slope_recv,
    inv_send, inv_recv, part_send, part_recv,
    qkv_core_send, qkv_core_recv, qkv_ring_send, qkv_ring_recv, qkv_half_send, qkv_half_recv,
    out_core_send, out_core_recv, out_ring_send, out_ring_recv, out_half_send, out_half_recv,
    gain_t_send, gain_t_recv, gain_d_send, gain_d_recv, load_sem, weight_sem, tile_sem,
):
    d, t, x, z = place()
    teacher, branch, own_hidden = part.at[0], part.at[1], part.at[2]
    parcel = [part.at[3], part.at[4]]
    arrived = [part.at[5], part.at[6]]
    dqkv = slope.at[:, :, pl.ds(0, 768)]
    dqkv_t = slope.at[pl.ds(0, 6), :, pl.ds(1024, 1024)]
    kept_hidden = slope.at[pl.ds(0, 4), :, pl.ds(2048, STRIPE)]
    tiles = slope.at[:, :, pl.ds(3072, 512)]

    loads = []

    def load(src, dst):
        copy = pltpu.make_async_copy(src, dst, load_sem.at[len(loads)])
        copy.start()
        loads.append(copy)
        return copy

    load_hidden = load(hidden_ref, own_hidden)
    load_teacher = load(teacher_ref, teacher)
    load_branch = load(branch_ref, branch)

    tensor_peers = [(d, lax.rem(t + k, N_TENSOR)) for k in range(1, N_TENSOR)]
    dp_peers = [(lax.rem(d + k, N_DP), t) for k in range(1, N_DP)]
    hidden_tree = TreeGather(hidden_ref, hidden_full, hidden_send, hidden_recv, 4)
    slope_tree = TreeGather(None, slope, slope_send, slope_recv, 2)
    tree = TreeScatter(part, slots, part_send, part_recv, 3)
    qkv = StageScatter(
        qkv_part, qkv_core, qkv_ring, qkv_half,
        (qkv_core_send, qkv_core_recv, qkv_ring_send, qkv_ring_recv, qkv_half_send.at[0], qkv_half_recv.at[0]),
    )
    out = StageScatter(
        out_part, out_core, out_ring, out_half,
        (out_core_send, out_core_recv, out_ring_send, out_ring_recv, out_half_send.at[0], out_half_recv.at[0]),
    )
    request[...] = jnp.broadcast_to(source_ref[...], (8, ROWS))
    greet(tensor_peers + dp_peers)

    def push_all(peers, src, dst, send, recv):
        copies = [remote(src, dst, send.at[k], recv.at[k], to) for k, to in enumerate(peers)]
        for copy in copies:
            copy.start()
        return copies

    source_copies = push_all(dp_peers, request, sources.at[d], source_send, source_recv)
    hidden_tree.begin()
    sources[d] = request[...]
    load_kept = load(hidden_ref, hidden_full.at[t])
    load_att = [load(att_in.at[pl.ds(s * ROWS, ROWS)], d_att.at[s]) for s in range(8)]
    load_w_out = [
        load(w_out_in.at[:, pl.ds(n * TILE, TILE)], qkv_part.at[n, pl.ds(0, 512)]) for n in range(16)
    ]
    load_qkv = [load(q_in, q_ref), load(k_in, k_ref), load(v_in, v_ref)]

    above = (
        lax.broadcasted_iota(jnp.int32, (ROWS, ROWS), 0) < lax.broadcasted_iota(jnp.int32, (ROWS, ROWS), 1)
    ).astype(bf16)
    slot_ids = lax.broadcasted_iota(jnp.int32, (SLOTS, ROWS), 0)
    peer_ids = lax.broadcasted_iota(jnp.int32, (N_DP, ROWS), 0)
    row_ids = lax.broadcasted_iota(jnp.int32, (ROWS, ROWS), 0)

    def slot_onehot(mask, rank, q):
        return ((slot_ids == rank[q:q + 1]) & (mask[q:q + 1] > 0)).astype(f32).astype(bf16)

    def ranks(mask):
        return jnp.dot(mask.astype(bf16), above, preferred_element_type=f32).astype(jnp.int32)

    from_peer = (peer_ids == lax.shift_right_logical(source_ref[...], 10)).astype(f32)
    from_rank = ranks(from_peer)
    place_rows = jnp.concatenate([slot_onehot(from_peer, from_rank, q) for q in range(N_DP)], axis=0)
    place_rows = place_rows.astype(f32).T.astype(bf16)

    for copy in source_copies:
        copy.wait_recv()
    wanted = jnp.concatenate([sources[q, 0:1, :] for q in range(N_DP)], axis=0)
    mine = (lax.shift_right_logical(wanted, 10) == d).astype(f32)
    rank = ranks(mine)
    local_row = jnp.bitwise_and(wanted, ROWS - 1)
    picks = []
    for q in range(N_DP):
        row_onehot = (row_ids == local_row[q:q + 1]).astype(f32).astype(bf16)
        picks.append(lax.dot_general(slot_onehot(mine, rank, q), row_onehot, NT, preferred_element_type=f32))
    load_teacher.wait()
    for b in (0, 1):
        pick = jnp.concatenate(picks[8 * b:8 * b + 8], axis=0).astype(bf16)
        for n in range(0, D, 512):
            columns = slice(n, n + 512)
            parcel[b][:, columns] = jnp.dot(pick, teacher[:, columns], preferred_element_type=f32).astype(bf16)

    def slot_rows(first, q):
        return part.at[first + lax.div(q, 8), pl.ds(pl.multiple_of(lax.rem(q, 8) * SLOTS, SLOTS), SLOTS)]

    parcel_copies = []
    for k, to in enumerate(dp_peers):
        copy = remote(slot_rows(3, to[0]), slot_rows(5, d), parcel_send.at[k], parcel_recv.at[k], to)
        copy.start()
        parcel_copies.append(copy)
    keep_own = load(slot_rows(3, d), slot_rows(5, d))

    load_hidden.wait()
    squares = jnp.zeros((ROWS, 128), f32)
    for n in range(0, D, 128):
        values = own_hidden[:, n:n + 128].astype(f32)
        squares = squares + values * values
    inv_rms = lax.rsqrt(jnp.sum(squares, axis=1, keepdims=True) * (1.0 / D) + eps_norm)
    inv_own[...] = jnp.broadcast_to(inv_rms, (ROWS, 128))
    inv_copies = push_all(tensor_peers, inv_own, inv_all.at[t], inv_send, inv_recv)
    inv_all[t] = inv_own[...]

    hidden_steps = hidden_tree.steps()
    for step in hidden_steps[:2]:
        step()

    seg_row = seg_ref[...].astype(f32)
    before = jnp.zeros_like(seg_row)
    for value in range(3):
        count = jnp.sum((seg_row == value).astype(f32), axis=1, keepdims=True)
        before = before + jnp.where(seg_row > value, count, 0.0)
    positions = lax.broadcasted_iota(jnp.int32, (1, GROUP), 1).astype(f32) - before
    for n in range(0, GROUP, 128):
        angles = freq_ref[...] * positions[:, n:n + 128]
        cos_ref[:, n:n + 128] = jnp.cos(angles)
        sin_ref[:, n:n + 128] = jnp.sin(angles)
    seg_col[...] = jnp.broadcast_to(seg_row, (128, GROUP)).T

    for step in hidden_steps[2:6]:
        step()
    for copy in load_att:
        copy.wait()
    for e in (0, 1):
        rows = jnp.concatenate([d_att[2 * i + e] for i in range(4)], axis=0)
        att_t[e] = rows.astype(f32).T.astype(bf16)
    for step in hidden_steps[6:8]:
        step()

    keep_own.wait()
    load_branch.wait()
    for copy in parcel_copies:
        copy.wait_recv()
    for n in range(0, D, 512):
        columns = slice(n, n + 512)
        target = jnp.dot(place_rows[:, :128], arrived[0][:, columns], preferred_element_type=f32)
        target += jnp.dot(place_rows[:, 128:], arrived[1][:, columns], preferred_element_type=f32)
        slope[t, :, columns] = ((branch[:, columns].astype(f32) - target) * (N_DP * GROUP) ** -0.5).astype(bf16)
    slope_tree.begin()
    slope_steps = slope_tree.steps()
    for step in hidden_steps[8:12] + slope_steps[:2] + hidden_steps[12:16] + slope_steps[2:8] + hidden_steps[16:20]:
        step()

    for step in slope_steps[8:18]:
        step()
    for copy in load_w_out:
        copy.wait()

    def slope_rows(e, columns):
        return jnp.concatenate([slope[2 * i + e, :, columns] for i in range(4)], axis=0)

    def attended_slope(e):
        def tile(n, carry):
            heads = pl.ds(pl.multiple_of(n * 256, 256), 256)
            value = jnp.zeros((512, 256), f32)
            for k in range(16):
                rows = slope_rows(e, slice(k * TILE, (k + 1) * TILE))
                value += lax.dot_general(rows, qkv_part[k, heads, :], NT, preferred_element_type=f32)
            value = value.astype(bf16)
            for i in range(4):
                d_att[2 * i + e, :, heads] = value[i * ROWS:(i + 1) * ROWS]
            return carry

        lax.fori_loop(0, 2, tile, 0)

    def out_gradient(e, first):
        def tile(n, carry):
            columns = pl.ds(pl.multiple_of(n * TILE, TILE), TILE)
            value = jnp.dot(att_t[e], slope_rows(e, columns), preferred_element_type=f32)
            if not first:
                value = value + out_part[n].astype(f32)
            out_part[n] = value.astype(bf16)
            return carry

        return tile

    attended_slope(z)
    lax.fori_loop(0, 16, out_gradient(z, True), 0)
    for step in slope_steps[18:]:
        step()
    attended_slope(1 - z)
    weight_copies = []
    for n in range(16):
        rows = pl.ds(n * TILE, TILE)
        for i, (src, dst) in enumerate((
            (wq_in.at[rows, pl.ds(0, 256)], qkv_part.at[n, pl.ds(0, 256)]),
            (wq_in.at[rows, pl.ds(256, 256)], qkv_part.at[n, pl.ds(256, 256)]),
            (wk_in.at[rows], qkv_part.at[n, pl.ds(512, 256), pl.ds(0, 128)]),
            (wv_in.at[rows], qkv_part.at[n, pl.ds(512, 256), pl.ds(128, 128)]),
        )):
            copy = pltpu.make_async_copy(src, dst, weight_sem.at[n, i])
            copy.start()
            weight_copies.append(copy)
    slope_tree.finish()
    lax.fori_loop(0, 16, out_gradient(1 - z, False), 0)
    for j in range(8):
        out.core_copy(j).start()
    for p in range(4):
        load(hidden_ref.at[:, pl.ds(p * STRIPE, STRIPE)], kept_hidden.at[p])

    for copy in load_qkv:
        copy.wait()
    blk = 256
    scale = HD ** -0.5
    dk_acc[...] = jnp.zeros_like(dk_acc)
    dv_acc[...] = jnp.zeros_like(dv_acc)
    k_t = k_ref[...].astype(f32).T.astype(bf16)

    def rotate_back(values, columns):
        u, w = values[:64], values[64:]
        c, s = cos_ref[:, columns], sin_ref[:, columns]
        return jnp.concatenate([u * c + w * s, w * c - u * s], axis=0)

    for i in range(GROUP // blk):
        rows = slice(i * blk, (i + 1) * blk)
        seen = (i + 1) * blk
        keys = jnp.concatenate([seg_col[:seen, :]] * 2, axis=1)
        allowed = (keys == seg_row[:, rows]) & (
            lax.broadcasted_iota(jnp.int32, (seen, blk), 0) <= lax.broadcasted_iota(jnp.int32, (seen, blk), 1) + i * blk
        )
        for h in range(4):
            cols = slice(h * HD, (h + 1) * HD)
            q = q_ref[rows, cols]
            da = d_att[2 * i:2 * i + 2, :, cols].reshape(blk, HD)
            scores = lax.dot_general(k_ref[:seen, :], q, NT, preferred_element_type=f32) * scale
            scores = jnp.where(allowed, scores, -1e30)
            weights = jnp.where(allowed, jnp.exp(scores - jnp.max(scores, axis=0, keepdims=True)), 0.0)
            soft = weights * (1.0 / jnp.sum(weights, axis=0, keepdims=True))
            d_probs = lax.dot_general(v_ref[:seen, :], da, NT, preferred_element_type=f32)
            delta = jnp.sum(soft * d_probs, axis=0, keepdims=True)
            d_scores = (soft * (d_probs - delta) * scale).astype(bf16)
            dv_acc[:seen, :] += jnp.dot(soft.astype(bf16), da, preferred_element_type=f32)
            dk_acc[:seen, :] += jnp.dot(d_scores, q, preferred_element_type=f32)
            dq_t = rotate_back(jnp.dot(k_t[:, :seen], d_scores, preferred_element_type=f32), rows)
            dqkv_t[h, :, rows] = dq_t.astype(bf16)
            dqkv[2 * i:2 * i + 2, :, cols] = dq_t.T.astype(bf16).reshape(2, ROWS, HD)
        if i == 1:
            out.begin_ring(0)
            out.begin_ring(1)
    dk_t = rotate_back(dk_acc[...].T, slice(0, GROUP))
    dqkv_t[4] = dk_t.astype(bf16)
    dqkv[:, :, 512:640] = dk_t.T.astype(bf16).reshape(8, ROWS, HD)
    dqkv_t[5] = dv_acc[...].T.astype(bf16)
    dqkv[:, :, 640:768] = dv_acc[...].astype(bf16).reshape(8, ROWS, HD)
    out.relay_ring(0)
    out.relay_ring(1)

    for copy in parcel_copies:
        copy.wait_send()
    for step in hidden_steps[20:]:
        step()
    for copy in inv_copies:
        copy.wait_recv()
    load_kept.wait()
    for copy in weight_copies:
        copy.wait()

    def tile_copy(n, slot):
        columns = pl.ds(pl.multiple_of(n * TILE, TILE), TILE)
        return pltpu.make_async_copy(hidden_full.at[:, :, columns], tiles.at[:, :, pl.ds(pl.multiple_of(slot * TILE, TILE), TILE)], tile_sem.at[slot])

    order = (0, 3, 1, 2)
    tile_copy(4 * order[0], 0).start()
    for g, p in enumerate(order):
        following = order[g + 1] if g < 3 else None

        def tile(i, carry, p=p, following=following):
            n = 4 * p + i
            slot = lax.rem(i, 2)
            if following is None:
                @pl.when(i < 3)
                def _():
                    tile_copy(n + 1, 1 - slot).start()
            else:
                tile_copy(n + 1 + lax.div(i + 1, 4) * (4 * (following - p) - 4), 1 - slot).start()
            tile_copy(n, slot).wait()
            columns = pl.ds(pl.multiple_of(n * TILE, TILE), TILE)
            inv = inv_all[...].reshape(GROUP, 128)
            held = tiles[:, :, pl.ds(pl.multiple_of(slot * TILE, TILE), TILE)]
            unit = held.reshape(GROUP, TILE).astype(f32) * jnp.concatenate([inv, inv], axis=1)
            normed = (unit * gain_ref[:, columns]).astype(bf16)
            grads = dqkv[...].reshape(GROUP, 768)
            total = lax.dot_general(grads[:, :256], qkv_part[n, :256, :], NT, preferred_element_type=f32)
            total += lax.dot_general(grads[:, 256:512], qkv_part[n, 256:512, :], NT, preferred_element_type=f32)
            total += lax.dot_general(grads[:, 512:], qkv_part[n, 512:, :], NT, preferred_element_type=f32)
            part[:, :, columns] = total.astype(bf16).reshape(8, ROWS, TILE)
            gain_sum[:, columns] = jnp.sum((total * unit).reshape(ROWS, 8, TILE), axis=0)
            qkv_part[n] = jnp.dot(
                dqkv_t[...].reshape(768, GROUP), normed, preferred_element_type=f32
            ).astype(bf16)
            return carry

        lax.fori_loop(0, 4, tile, 0)
        if p >= tree.over_z:
            tree.begin_z(p)
        else:
            tree.begin_x(1, p)
            tree.begin_x(0, p)
        qkv.core_copy(2 * p).start()
        qkv.core_copy(2 * p + 1).start()

    gain_row = jnp.sum(gain_sum[...], axis=0, keepdims=True)
    for i in range(32):
        gain_block[0, i:i + 1, :] = gain_row[:, i * 128:(i + 1) * 128]
    gain_tensor[t] = gain_block[0]
    gain_copies = push_all(tensor_peers, gain_block.at[0], gain_tensor.at[t], gain_t_send, gain_t_recv)

    tree.relay(1, 0)
    tree.relay(0, 0)
    qkv.begin_ring(0)
    qkv.begin_ring(1)
    tree.relay(1, 1)
    tree.relay(0, 1)
    tree.z_done(2, 3)
    tree.z_done(3, 3)
    tree.begin_x(0, 3)
    qkv.relay_ring(0)
    tree.root_other(0)
    tree.relay(1, 2)
    tree.relay(0, 2)
    qkv.relay_ring(1)
    tree.z_done(1, 3)
    tree.root_other(1)
    out.send_half()

    for copy in gain_copies:
        copy.wait_recv()
    gain_total = gain_tensor[0]
    for k in range(1, N_TENSOR):
        gain_total = gain_total + gain_tensor[k]
    gain_block[1] = gain_total
    gain_dp[d] = gain_total
    dp_copies = push_all(dp_peers, gain_block.at[1], gain_dp.at[d], gain_d_send, gain_d_recv)

    tree.relay(0, 3)
    tree.z_done(0, 3)
    tree.root_other(2)
    qkv.send_half()
    for b, value in enumerate(out.result()):
        gout_ref[b * 256:(b + 1) * 256, :] = value

    for copy in dp_copies:
        copy.wait_recv()
    gain_total = gain_dp[0]
    for k in range(1, N_DP):
        gain_total = gain_total + gain_dp[k]
    ggain_ref[...] = gain_total

    for copy in loads[-4:]:
        copy.wait()
    inv = inv_own[:, 0:1]
    dots = jnp.zeros((ROWS, 1), f32)
    for p in (0, 1, 3, 2):
        columns = slice(p * STRIPE, (p + 1) * STRIPE)
        scaled = tree.result(p) * gain_ref[:, columns]
        dh_ref[:, columns] = scaled
        unit = kept_hidden[p].astype(f32) * inv
        dots = dots + jnp.sum(scaled * unit, axis=1, keepdims=True)
    mean = dots * (1.0 / D)
    for p in range(4):
        columns = slice(p * STRIPE, (p + 1) * STRIPE)
        unit = kept_hidden[p].astype(f32) * inv
        dh_ref[:, columns] = inv * (dh_ref[:, columns] - unit * mean)
    top, bottom = qkv.result()
    gq_ref[:, :384] = top.T
    gq_ref[:, 384:] = bottom[:128].T
    gk_ref[...] = bottom[128:256].T
    gv_ref[...] = bottom[256:].T

    hidden_tree.finish()
    tree.finish()
    out.finish()
    qkv.finish()
    for copy in source_copies + inv_copies + gain_copies + dp_copies:
        copy.wait_send()


def per_device(
    hidden_in, teacher, row_source, segments, branch, queries, key_rot, value_rows, attended, norm_gain,
    w_query, w_key, w_value, w_out,
):
    any_space = pl.BlockSpec(memory_space=pl.ANY)
    vmem = pl.BlockSpec(memory_space=pltpu.VMEM)
    dma = pltpu.SemaphoreType.DMA
    scratch = pltpu.VMEM
    frequency = (theta_base ** (-2.0 * np.arange(HD // 2, dtype=np.float64) / HD)).astype(np.float32)
    frequency = np.broadcast_to(frequency[:, None], (HD // 2, 128))
    stage_sems = [dma((8,)), dma((8,)), dma((2, 6)), dma((2, 6)), dma((1,)), dma((1,))]
    shape = jax.ShapeDtypeStruct
    d_hidden, grad_query, grad_key, grad_value, grad_out, grad_gain, _ = pl.pallas_call(
        kernel,
        out_shape=(
            shape((ROWS, D), f32), shape((256, 512), f32), shape((256, 128), f32), shape((256, 128), f32),
            shape((512, 256), f32), shape((32, 128), f32), shape((N_TENSOR, ROWS, D), bf16),
        ),
        in_specs=[vmem] * 4 + [any_space] * 11,
        out_specs=(vmem,) * 6 + (any_space,),
        scratch_shapes=[
            scratch((8, ROWS, D), bf16), scratch((8, ROWS, D), bf16), scratch((28, ROWS, STRIPE), bf16),
            scratch((16, 768, 256), bf16), scratch((8, 768, 256), bf16), scratch((2, 6, 384, 256), bf16), scratch((768, 256), bf16),
            scratch((16, 512, 256), bf16), scratch((8, 512, 256), bf16), scratch((2, 6, 256, 256), bf16), scratch((512, 256), bf16),
            scratch((2, 512, 512), bf16), scratch((8, ROWS, 512), bf16),
            scratch((GROUP, 512), bf16), scratch((GROUP, HD), bf16), scratch((GROUP, HD), bf16),
            scratch((HD // 2, GROUP), f32), scratch((HD // 2, GROUP), f32), scratch((GROUP, 128), f32),
            scratch((ROWS, 128), f32), scratch((N_TENSOR, ROWS, 128), f32),
            scratch((GROUP, HD), f32), scratch((GROUP, HD), f32),
            scratch((8, ROWS), jnp.int32), scratch((N_DP, 8, ROWS), jnp.int32),
            scratch((8, D), f32), scratch((2, 32, 128), f32), scratch((N_TENSOR, 32, 128), f32), scratch((N_DP, 32, 128), f32),
            dma((15,)), dma((15,)), dma((15,)), dma((15,)),
            dma((28,)), dma((8, 4)), dma((28,)), dma((8, 4)),
            dma((7,)), dma((7,)), dma((28,)), dma((28,)),
        ] + stage_sems + stage_sems + [
            dma((7,)), dma((7,)), dma((15,)), dma((15,)), dma((40,)), dma((16, 4)), dma((2,)),
        ],
        compiler_params=pltpu.CompilerParams(
            collective_id=1, has_side_effects=True, vmem_limit_bytes=60 * 2**20
        ),
        cost_estimate=pl.CostEstimate(flops=27 * 10**9, bytes_accessed=60 * 2**20, transcendentals=4 * 2**20),
    )(
        row_source[None, :], segments, frequency, norm_gain[None, :], teacher, branch, hidden_in, queries, key_rot, value_rows,
        attended, w_query, w_key, w_value, w_out,
    )
    return (grad_query, grad_key, grad_value, grad_out, grad_gain.reshape(D), d_hidden)


def solution(mesh):
    return jax.shard_map(
        per_device,
        mesh=mesh,
        in_specs=(
            P(("dp", "tensor"), None),
            P(("dp", "tensor"), None),
            P(("dp", "tensor")),
            P("dp", None),
            P(("dp", "tensor"), None),
            P("dp", "tensor"),
            P("dp", "tensor"),
            P("dp", "tensor"),
            P("dp", "tensor"),
            P(),
            P(None, "tensor"),
            P(None, "tensor"),
            P(None, "tensor"),
            P("tensor", None),
        ),
        out_specs=(
            P("dp", "tensor"),
            P("dp", "tensor"),
            P("dp", "tensor"),
            P("tensor", "dp"),
            P(),
            P(("dp", "tensor"), None),
        ),
        check_vma=False,
    )
```

```python
import jax
import jax.numpy as jnp
import numpy as np
from jax import lax
from jax.experimental import pallas as pl
from jax.experimental.pallas import tpu as pltpu
from jax.sharding import PartitionSpec as P

HEADS = 32
KVH = 8
HD = 128
D = 4096
ROWS = 128
GROUP = 1024
N_DP = 16
N_TENSOR = 8
CAPACITY = 9
CHUNK = 512
SLOTS = 80
PIECE = 32
STRIPE = 1024
TILE = 256

MESH = pl.DeviceIdType.MESH
f32 = jnp.float32
bf16 = jnp.bfloat16
NT = (((1,), (1,)), ((), ()))

theta_base = 500000.0
eps_norm = 1e-05


def place():
    d, t = lax.axis_index("dp"), lax.axis_index("tensor")
    return d, t, lax.div(t, 2), lax.rem(t, 2)


def tensor_index(x, z):
    return x * 2 + z


def greet(ids):
    barrier = pltpu.get_barrier_semaphore()
    for device in ids:
        pl.semaphore_signal(barrier, inc=1, device_id=device, device_id_type=MESH)
    pl.semaphore_wait(barrier, len(ids))


def remote(src, dst, send_sem, recv_sem, to):
    return pltpu.make_async_remote_copy(
        src_ref=src, dst_ref=dst, send_sem=send_sem, recv_sem=recv_sem, device_id=to, device_id_type=MESH
    )


class TreeGather:
    def __init__(self, own, full, send, recv, over_z):
        self.over_z = over_z
        self.own, self.full, self.send_sems, self.recv_sems = own, full, send, recv
        self.d, self.t, self.x, self.z = place()
        self.copies = []
        d, x, z = self.d, self.x, self.z
        right, left, across, other = lax.rem(x + 1, 4), lax.rem(x + 3, 4), lax.rem(x + 2, 4), 1 - z
        self.to_right = (d, tensor_index(right, z))
        self.to_left = (d, tensor_index(left, z))
        self.to_z = (d, tensor_index(x, other))
        self.near = [tensor_index(x, other), tensor_index(left, z), tensor_index(right, z), tensor_index(across, z)]
        self.far = [tensor_index(left, other), tensor_index(right, other), tensor_index(across, other)]

    def piece(self, s, p):
        return self.full.at[s, pl.ds(p * PIECE, PIECE)]

    def send(self, s, p, to, own=False):
        src = self.own.at[pl.ds(p * PIECE, PIECE)] if own else self.piece(s, p)
        copy = remote(src, self.piece(s, p), self.send_sems.at[len(self.copies)], self.recv_sems.at[s, p], to)
        copy.start()
        self.copies.append(copy)

    def wait(self, s, p):
        piece = self.piece(s, p)
        remote(piece, piece, self.send_sems.at[0], self.recv_sems.at[s, p], self.to_z).wait_recv()

    def begin(self):
        by_z = list(range(4))
        by_x = list(range(self.over_z, 4)) + list(range(self.over_z))
        for i in (0, 2):
            a, b = by_x[i:i + 2]
            for p, to in (
                (by_z[i], self.to_z), (a, self.to_right), (b, self.to_left), (by_z[i + 1], self.to_z),
                (b, self.to_right), (a, self.to_left),
            ):
                if to is not self.to_z or p < self.over_z or self.over_z < 4:
                    self.send(self.t, p, to, self.own is not None)

    def steps(self):
        partner, left, right, across = self.near
        far_left, far_right, far_across = self.far
        first = list(range(self.over_z))
        last = list(range(self.over_z, 4))
        order = [(partner, p) for p in first[:2]] + [(s, p) for p in (last + first)[:2] for s in (left, right)]
        order += [(partner, p) for p in first[2:]] + [(s, p) for p in (last + first)[2:] for s in (left, right)]
        order += [(s, p) for p in first for s in (far_left, far_right)] + [(across, p) for p in last + first]
        order += [(far_across, p) for p in first]
        order += [(s, p) for s in (partner, far_left, far_right, far_across) for p in last]

        def targets_of(s, p):
            targets = []
            if s is partner and p < self.over_z:
                targets += [self.to_right, self.to_left]
            if s is left and p % 2 == 0 or s is far_left and p % 2 == 0 and p < self.over_z:
                targets.append(self.to_right)
            if s is right and p % 2 == 1 or s is far_right and p % 2 == 1 and p < self.over_z:
                targets.append(self.to_left)
            if p >= self.over_z and (s is left or s is right or s is across):
                targets.append(self.to_z)
            return targets

        plan = [(s, p, targets_of(s, p)) for s, p in order]

        def make(s, p, targets):
            def step():
                self.wait(s, p)
                for to in targets:
                    self.send(s, p, to)
            return step

        roles = {id(s): name for s, name in (
            (partner, "partner"), (left, "left"), (right, "right"), (across, "across"),
            (far_left, "far_left"), (far_right, "far_right"), (far_across, "far_across"),
        )}
        return {(roles[id(s)], p): make(s, p, targets) for s, p, targets in plan}

    def finish(self):
        for copy in self.copies:
            copy.wait_send()


class TreeScatter:
    def __init__(self, part, slots, send, recv, over_z):
        self.over_z = over_z
        first, last = range(over_z), range(over_z, 4)
        self.part, self.slots, self.send_sems, self.recv_sems = part, slots, send, recv
        self.d, self.t, self.x, self.z = place()
        d, x, z = self.d, self.x, self.z
        self.to_right = (d, tensor_index(lax.rem(x + 1, 4), z))
        self.to_left = (d, tensor_index(lax.rem(x + 3, 4), z))
        self.to_z = (d, tensor_index(x, 1 - z))
        names = [(kind, e, p) for e in (0, 1) for p in first for kind in ("relay", "right", "left")]
        names += [("z", 0, p) for p in first]
        names += [("zz", k, p) for k in range(4) for p in last]
        names += [(kind, 0, p) for p in last for kind in ("relay", "right", "left")]
        self.index = {name: n for n, name in enumerate(names)}
        self.copies = []

    def dest(self, k, e):
        z = self.z if e == 0 else 1 - self.z
        return tensor_index(lax.rem(self.x + k, 4), z)

    def stripe(self, p):
        return pl.ds(p * STRIPE, STRIPE)

    def send(self, k, e, p, to, name):
        n = self.index[name]
        copy = remote(
            self.part.at[self.dest(k, e), :, self.stripe(p)], self.slots.at[n], self.send_sems.at[len(self.copies)],
            self.recv_sems.at[n], to,
        )
        copy.start()
        self.copies.append(copy)

    def wait(self, name):
        n = self.index[name]
        slot = self.slots.at[n]
        remote(slot, slot, self.send_sems.at[0], self.recv_sems.at[n], self.to_z).wait_recv()

    def total(self, k, e, p, names):
        for name in names:
            self.wait(name)
        total = self.part[self.dest(k, e), :, self.stripe(p)].astype(f32)
        for name in names:
            total = total + self.slots[self.index[name]].astype(f32)
        return total

    def add(self, k, e, p, names):
        self.part[self.dest(k, e), :, self.stripe(p)] = self.total(k, e, p, names).astype(bf16)

    def begin_z(self, p):
        for k in (2, 1, 3, 0):
            self.send(k, 1, p, self.to_z, ("zz", k, p))

    def begin_x(self, e, p):
        if p % 2 == 0:
            self.send(2, e, p, self.to_left, ("relay", e, p))
            self.send(1, e, p, self.to_right, ("left", e, p))
        else:
            self.send(2, e, p, self.to_right, ("relay", e, p))
            self.send(3, e, p, self.to_left, ("right", e, p))

    def relay(self, e, p):
        if p % 2 == 0:
            self.add(3, e, p, [("relay", e, p)])
            self.send(3, e, p, self.to_left, ("right", e, p))
        else:
            self.add(1, e, p, [("relay", e, p)])
            self.send(1, e, p, self.to_right, ("left", e, p))

    def z_done(self, k, p):
        self.add(k, 0, p, [("zz", k, p)])

    def root_other(self, p):
        self.add(0, 1, p, [("right", 1, p), ("left", 1, p)])
        self.send(0, 1, p, self.to_z, ("z", 0, p))

    def result(self, p):
        names = [("right", 0, p), ("left", 0, p)]
        return self.total(0, 0, p, names + [("z", 0, p)] if p < self.over_z else names)

    def finish(self):
        for copy in self.copies:
            copy.wait_send()


class StageScatter:
    def __init__(self, part, core, ring, half, sems):
        self.part, self.core, self.ring, self.half = part, core, ring, half
        self.core_send, self.core_recv, self.ring_send, self.ring_recv, self.half_send, self.half_recv = sems
        d, t, _, _ = place()
        self.c, self.y, self.zh = lax.rem(d, 2), lax.rem(lax.div(d, 2), 4), lax.div(d, 8)
        self.to_core = (d + 1 - 2 * self.c, t)
        self.to_right = ((self.zh * 4 + lax.rem(self.y + 1, 4)) * 2 + self.c, t)
        self.to_left = ((self.zh * 4 + lax.rem(self.y + 3, 4)) * 2 + self.c, t)
        self.to_half = (((1 - self.zh) * 4 + self.y) * 2 + self.c, t)
        self.cut = core.shape[1] // 2
        self.copies = []

    def core_copy(self, j):
        return remote(
            self.part.at[2 * j + 1 - self.c], self.core.at[j], self.core_send.at[j], self.core_recv.at[j], self.to_core
        )

    def block(self, k, half):
        return 2 * (half * 4 + lax.rem(self.y + k, 4)) + self.c

    def fold_core(self, k, half):
        n = self.block(k, half)
        j = lax.div(n, 2)
        self.core_copy(j).wait_recv()
        self.part[n] = (self.part[n].astype(f32) + self.core[j].astype(f32)).astype(bf16)

    def rows(self, b):
        return pl.ds(b * self.cut, self.cut)

    def send(self, k, half, b, to, slot):
        copy = remote(
            self.part.at[self.block(k, half), self.rows(b)], self.ring.at[half, slot],
            self.ring_send.at[half, slot], self.ring_recv.at[half, slot], to,
        )
        copy.start()
        self.copies.append(copy)

    def wait(self, half, slot):
        ref = self.ring.at[half, slot]
        remote(ref, ref, self.ring_send.at[half, slot], self.ring_recv.at[half, slot], self.to_core).wait_recv()

    def begin_ring(self, half):
        self.fold_core(2, half)
        self.send(2, half, 0, self.to_left, 0)
        self.send(2, half, 1, self.to_right, 1)
        self.fold_core(1, half)
        self.send(1, half, 0, self.to_right, 2)
        self.fold_core(3, half)
        self.send(3, half, 1, self.to_left, 5)
        self.fold_core(0, half)

    def relay_ring(self, half):
        for k, b, slot, to, target in ((3, 0, 0, self.to_left, 4), (1, 1, 1, self.to_right, 3)):
            self.wait(half, slot)
            n = self.block(k, half)
            total = self.part[n, self.rows(b)].astype(f32) + self.ring[half, slot].astype(f32)
            self.part[n, self.rows(b)] = total.astype(bf16)
            self.send(k, half, b, to, target)

    def ring_total(self, half, b):
        total = self.part[self.block(0, half), self.rows(b)].astype(f32)
        for slot in (2 + b, 4 + b):
            self.wait(half, slot)
            total = total + self.ring[half, slot].astype(f32)
        return total

    def send_half(self):
        n = self.block(0, 1 - self.zh)
        for b in (0, 1):
            self.part[n, self.rows(b)] = self.ring_total(1 - self.zh, b).astype(bf16)
        copy = remote(self.part.at[n], self.half, self.half_send, self.half_recv, self.to_half)
        copy.start()
        self.half_copy = copy

    def result(self):
        totals = [self.ring_total(self.zh, b) for b in (0, 1)]
        self.half_copy.wait_recv()
        return [total + self.half[self.rows(b), :].astype(f32) for b, total in enumerate(totals)]

    def finish(self):
        for copy in self.copies:
            copy.wait_send()
        self.half_copy.wait_send()
        for j in range(8):
            self.core_copy(j).wait_send()


def kernel(
    source_ref, seg_ref, gain_ref, teacher_ref, branch_ref, hidden_ref, q_in, k_in, v_in, att_in, wq_in, wk_in,
    wv_in, w_out_in,
    dh_ref, gq_ref, gk_ref, gv_ref, gout_ref, ggain_ref, hidden_full,
    part, slope, slots, qkv_part, qkv_core, qkv_ring, qkv_half, out_part, out_core, out_ring, out_half,
    att_t, d_att, q_ref, k_ref, v_ref, cos_ref, sin_ref, seg_col, inv_own, inv_all, dk_acc, dv_acc,
    request, sources, gain_sum, gain_block, gain_tensor, gain_dp,
    source_send, source_recv, parcel_send, parcel_recv, hidden_send, hidden_recv, slope_send, slope_recv,
    inv_send, inv_recv, part_send, part_recv,
    qkv_core_send, qkv_core_recv, qkv_ring_send, qkv_ring_recv, qkv_half_send, qkv_half_recv,
    out_core_send, out_core_recv, out_ring_send, out_ring_recv, out_half_send, out_half_recv,
    gain_t_send, gain_t_recv, gain_d_send, gain_d_recv, load_sem, weight_sem, tile_sem,
):
    d, t, x, z = place()
    teacher, branch, own_hidden = part.at[0], part.at[1], part.at[2]
    dqkv = slope.at[:, :, pl.ds(0, 768)]
    dqkv_t = slope.at[pl.ds(0, 6), :, pl.ds(1024, 1024)]
    kept_hidden = slope.at[pl.ds(0, 4), :, pl.ds(2048, STRIPE)]
    tiles = slope.at[:, :, pl.ds(3072, 512)]

    loads = []

    def load(src, dst):
        copy = pltpu.make_async_copy(src, dst, load_sem.at[len(loads)])
        copy.start()
        loads.append(copy)
        return copy

    load_hidden = load(hidden_ref, own_hidden)
    load_teacher = load(teacher_ref, teacher)
    load_branch = load(branch_ref, branch)

    tensor_peers = [(d, lax.rem(t + k, N_TENSOR)) for k in range(1, N_TENSOR)]
    dp_peers = [(lax.rem(d + k, N_DP), t) for k in range(1, N_DP)]
    hidden_tree = TreeGather(hidden_ref, hidden_full, hidden_send, hidden_recv, 3)
    slope_tree = TreeGather(None, slope, slope_send, slope_recv, 2)
    tree = TreeScatter(part, slots, part_send, part_recv, 3)
    qkv = StageScatter(
        qkv_part, qkv_core, qkv_ring, qkv_half,
        (qkv_core_send, qkv_core_recv, qkv_ring_send, qkv_ring_recv, qkv_half_send.at[0], qkv_half_recv.at[0]),
    )
    out = StageScatter(
        out_part, out_core, out_ring, out_half,
        (out_core_send, out_core_recv, out_ring_send, out_ring_recv, out_half_send.at[0], out_half_recv.at[0]),
    )
    request[...] = jnp.broadcast_to(source_ref[...], (8, ROWS))
    greet(tensor_peers + dp_peers)

    def push_all(peers, src, dst, send, recv):
        copies = [remote(src, dst, send.at[k], recv.at[k], to) for k, to in enumerate(peers)]
        for copy in copies:
            copy.start()
        return copies

    source_copies = push_all(dp_peers, request, sources.at[d], source_send, source_recv)
    hidden_tree.begin()
    sources[d] = request[...]
    load_att = [load(att_in.at[pl.ds(s * ROWS, ROWS)], d_att.at[s]) for s in range(8)]
    load_w_out = [
        load(w_out_in.at[:, pl.ds(n * TILE, TILE)], qkv_part.at[n, pl.ds(0, 512)]) for n in range(16)
    ]
    load_qkv = [load(q_in, q_ref), load(k_in, k_ref), load(v_in, v_ref)]

    above = (
        lax.broadcasted_iota(jnp.int32, (ROWS, ROWS), 0) < lax.broadcasted_iota(jnp.int32, (ROWS, ROWS), 1)
    ).astype(bf16)
    block_row = lax.broadcasted_iota(jnp.int32, (SLOTS, ROWS), 0)
    chunk_ids = lax.shift_right_logical(block_row * 57, 9)
    slot_ids = block_row - CAPACITY * chunk_ids
    peer_ids = lax.broadcasted_iota(jnp.int32, (N_DP, ROWS), 0)
    row_ids = lax.broadcasted_iota(jnp.int32, (ROWS, ROWS), 0)

    def slot_onehot(mask, rank, q):
        return ((slot_ids == rank[q:q + 1]) & (mask[q:q + 1] > 0)).astype(f32).astype(bf16)

    def ranks(mask):
        return jnp.dot(mask.astype(bf16), above, preferred_element_type=f32).astype(jnp.int32)

    from_peer = (peer_ids == lax.shift_right_logical(source_ref[...], 10)).astype(f32)
    taken = jnp.sum(from_peer * (SLOTS * peer_ids + ranks(from_peer)).astype(f32), axis=0, keepdims=True)
    taken = jnp.concatenate([jnp.broadcast_to(taken, (ROWS, ROWS)).T] * 10, axis=1)
    lanes = lax.broadcasted_iota(jnp.int32, (ROWS, N_DP * SLOTS), 1).astype(f32)
    for k in range(8):
        onehot = (lanes == taken + CAPACITY * k).astype(f32).astype(bf16)
        for n in range(5):
            out_part[2 * n + k // 4, (k % 4) * ROWS:(k % 4 + 1) * ROWS, :] = onehot[:, n * TILE:(n + 1) * TILE]

    for copy in source_copies:
        copy.wait_recv()
    wanted = jnp.concatenate([sources[q, 0:1, :] for q in range(N_DP)], axis=0)
    mine = (lax.shift_right_logical(wanted, 10) == d).astype(f32)
    rank = ranks(mine)
    local_row = jnp.bitwise_and(wanted, ROWS - 1)
    picks = []
    for q in range(N_DP):
        row_onehot = (row_ids == local_row[q:q + 1]).astype(f32).astype(bf16)
        picks.append(lax.dot_general(slot_onehot(mine, rank, q), row_onehot, NT, preferred_element_type=f32))
    load_teacher.wait()
    chunks = jnp.concatenate([teacher[:, k * CHUNK:(k + 1) * CHUNK] for k in range(8)], axis=0)
    for b in range(4):
        pick = jnp.concatenate([
            jnp.concatenate([jnp.where(chunk_ids == k, picks[q], 0.0).astype(bf16) for k in range(8)], axis=1)
            for q in range(4 * b, 4 * b + 4)
        ], axis=0)
        values = jnp.dot(pick, chunks, preferred_element_type=f32).astype(bf16)
        for i in range(4):
            q = 4 * b + i
            part[3 + q // 8, :SLOTS, (q % 8) * CHUNK:(q % 8 + 1) * CHUNK] = values[i * SLOTS:(i + 1) * SLOTS]

    def slot_rows(first, q):
        columns = pl.ds(pl.multiple_of(lax.rem(q, 8) * CHUNK, CHUNK), CHUNK)
        return part.at[first + lax.div(q, 8), pl.ds(0, SLOTS), columns]

    parcel_copies = []
    for k, to in enumerate(dp_peers):
        copy = remote(slot_rows(3, to[0]), slot_rows(5, d), parcel_send.at[k], parcel_recv.at[k], to)
        copy.start()
        parcel_copies.append(copy)
    keep_own = load(slot_rows(3, d), slot_rows(5, d))

    load_hidden.wait()
    load_kept = load(own_hidden, hidden_full.at[t])
    squares = jnp.zeros((ROWS, 128), f32)
    for n in range(0, D, 128):
        values = own_hidden[:, n:n + 128].astype(f32)
        squares = squares + values * values
    inv_rms = lax.rsqrt(jnp.sum(squares, axis=1, keepdims=True) * (1.0 / D) + eps_norm)
    inv_own[...] = jnp.broadcast_to(inv_rms, (ROWS, 128))
    inv_copies = push_all(tensor_peers, inv_own, inv_all.at[t], inv_send, inv_recv)
    inv_all[t] = inv_own[...]

    hidden_steps = hidden_tree.steps()
    slope_steps = slope_tree.steps()

    def take(steps, *names):
        for role, p in names:
            steps.pop((role, p))()

    take(hidden_steps, ("partner", 0), ("left", 3), ("right", 3), ("left", 0))

    seg_row = seg_ref[...].astype(f32)
    before = jnp.zeros_like(seg_row)
    for value in range(3):
        count = jnp.sum((seg_row == value).astype(f32), axis=1, keepdims=True)
        before = before + jnp.where(seg_row > value, count, 0.0)
    positions = lax.broadcasted_iota(jnp.int32, (1, GROUP), 1).astype(f32) - before
    steps_down = lax.broadcasted_iota(jnp.int32, (HD // 2, 128), 0).astype(f32)
    frequency = jnp.exp(steps_down * float(-2.0 * np.log(theta_base) / HD))
    for n in range(0, GROUP, 128):
        angles = frequency * positions[:, n:n + 128]
        cos_ref[:, n:n + 128] = jnp.cos(angles)
        sin_ref[:, n:n + 128] = jnp.sin(angles)
    seg_col[...] = jnp.broadcast_to(seg_row, (128, GROUP)).T

    take(hidden_steps, ("partner", 1), ("right", 1))
    for copy in load_att:
        copy.wait()
    for e in (0, 1):
        rows = jnp.concatenate([d_att[2 * i + e] for i in range(4)], axis=0)
        att_t[e] = rows.astype(f32).T.astype(bf16)
    take(hidden_steps, ("left", 2))

    keep_own.wait()
    load_branch.wait()
    for copy in parcel_copies:
        copy.wait_recv()
    came = jnp.concatenate(
        [part[5 + q // 8, :SLOTS, (q % 8) * CHUNK:(q % 8 + 1) * CHUNK] for q in range(N_DP)], axis=0
    )
    for b in (0, 1):
        onehot = jnp.concatenate([out_part[2 * n + b] for n in range(5)], axis=1)
        target = jnp.dot(onehot, came, preferred_element_type=f32)
        for i in range(4):
            columns = slice((4 * b + i) * CHUNK, (4 * b + i + 1) * CHUNK)
            change = branch[:, columns].astype(f32) - target[i * ROWS:(i + 1) * ROWS]
            slope[t, :, columns] = (change * (N_DP * GROUP) ** -0.5).astype(bf16)
    slope_tree.begin()
    for copy in parcel_copies:
        copy.wait_send()

    for copy in load_qkv:
        copy.wait()
    blk = 256
    scale = HD ** -0.5

    def forward(i):
        rows = slice(i * blk, (i + 1) * blk)
        seen = (i + 1) * blk
        keys = jnp.concatenate([seg_col[:seen, :]] * 2, axis=1)
        allowed = (keys == seg_row[:, rows]) & (
            lax.broadcasted_iota(jnp.int32, (seen, blk), 0) <= lax.broadcasted_iota(jnp.int32, (seen, blk), 1) + i * blk
        )
        for h in range(4):
            scores = lax.dot_general(
                k_ref[:seen, :], q_ref[rows, h * HD:(h + 1) * HD], NT, preferred_element_type=f32
            ) * scale
            scores = jnp.where(allowed, scores, -1e30)
            weights = jnp.where(allowed, jnp.exp(scores - jnp.max(scores, axis=0, keepdims=True)), 0.0)
            soft = (weights * (1.0 / jnp.sum(weights, axis=0, keepdims=True))).astype(bf16)
            first = (4 * i + h) * blk
            part[:2 * (i + 1), :, first:first + blk] = soft.reshape(2 * (i + 1), ROWS, blk)

    load_kept.wait()
    take(hidden_steps, ("far_left", 0), ("far_right", 1), ("across", 3))
    forward(0)
    take(slope_steps, ("partner", 0), ("partner", 1))
    forward(1)
    take(slope_steps, ("left", 2), ("right", 3), ("left", 3), ("right", 2))
    forward(2)
    take(slope_steps, ("left", 0), ("right", 1))
    take(hidden_steps, ("partner", 2))
    take(slope_steps, ("far_left", 0), ("far_right", 1))
    forward(3)

    for p in (2, 3, 0, 1):
        take(slope_steps, ("across", p))
    take(slope_steps, ("left", 1), ("right", 0))
    for copy in load_w_out:
        copy.wait()

    def slope_rows(e, columns):
        return jnp.concatenate([slope[2 * i + e, :, columns] for i in range(4)], axis=0)

    def attended_slope(e):
        def tile(n, carry):
            heads = pl.ds(pl.multiple_of(n * 256, 256), 256)
            value = jnp.zeros((512, 256), f32)
            for k in range(16):
                rows = slope_rows(e, slice(k * TILE, (k + 1) * TILE))
                value += lax.dot_general(rows, qkv_part[k, heads, :], NT, preferred_element_type=f32)
            value = value.astype(bf16)
            for i in range(4):
                d_att[2 * i + e, :, heads] = value[i * ROWS:(i + 1) * ROWS]
            return carry

        lax.fori_loop(0, 2, tile, 0)

    def out_gradient(e, first):
        def tile(n, carry):
            columns = pl.ds(pl.multiple_of(n * TILE, TILE), TILE)
            value = jnp.dot(att_t[e], slope_rows(e, columns), preferred_element_type=f32)
            if not first:
                value = value + out_part[n].astype(f32)
            out_part[n] = value.astype(bf16)
            return carry

        return tile

    attended_slope(z)
    lax.fori_loop(0, 16, out_gradient(z, True), 0)
    take(hidden_steps, ("far_left", 2))
    for step in slope_steps.values():
        step()
    attended_slope(1 - z)
    weight_copies = []
    for n in range(16):
        rows = pl.ds(n * TILE, TILE)
        for i, (src, dst) in enumerate((
            (wq_in.at[rows, pl.ds(0, 256)], qkv_part.at[n, pl.ds(0, 256)]),
            (wq_in.at[rows, pl.ds(256, 256)], qkv_part.at[n, pl.ds(256, 256)]),
            (wk_in.at[rows], qkv_part.at[n, pl.ds(512, 256), pl.ds(0, 128)]),
            (wv_in.at[rows], qkv_part.at[n, pl.ds(512, 256), pl.ds(128, 128)]),
        )):
            copy = pltpu.make_async_copy(src, dst, weight_sem.at[n, i])
            copy.start()
            weight_copies.append(copy)
    slope_tree.finish()
    lax.fori_loop(0, 16, out_gradient(1 - z, False), 0)
    for j in range(8):
        out.core_copy(j).start()
    for p in range(4):
        load(hidden_ref.at[:, pl.ds(p * STRIPE, STRIPE)], kept_hidden.at[p])

    dk_acc[...] = jnp.zeros_like(dk_acc)
    dv_acc[...] = jnp.zeros_like(dv_acc)
    k_t = k_ref[...].astype(f32).T.astype(bf16)

    def rotate_back(values, columns):
        u, w = values[:64], values[64:]
        c, s = cos_ref[:, columns], sin_ref[:, columns]
        return jnp.concatenate([u * c + w * s, w * c - u * s], axis=0)

    for i in range(GROUP // blk):
        rows = slice(i * blk, (i + 1) * blk)
        seen = (i + 1) * blk
        for h in range(4):
            cols = slice(h * HD, (h + 1) * HD)
            q = q_ref[rows, cols]
            da = d_att[2 * i:2 * i + 2, :, cols].reshape(blk, HD)
            first = (4 * i + h) * blk
            probs = part[:2 * (i + 1), :, first:first + blk].reshape(seen, blk)
            soft = probs.astype(f32)
            d_probs = lax.dot_general(v_ref[:seen, :], da, NT, preferred_element_type=f32)
            delta = jnp.sum(soft * d_probs, axis=0, keepdims=True)
            d_scores = (soft * (d_probs - delta) * scale).astype(bf16)
            dv_acc[:seen, :] += jnp.dot(probs, da, preferred_element_type=f32)
            dk_acc[:seen, :] += jnp.dot(d_scores, q, preferred_element_type=f32)
            dq_t = rotate_back(jnp.dot(k_t[:, :seen], d_scores, preferred_element_type=f32), rows)
            dqkv_t[h, :, rows] = dq_t.astype(bf16)
            dqkv[2 * i:2 * i + 2, :, cols] = dq_t.T.astype(bf16).reshape(2, ROWS, HD)
        if i == 1:
            out.begin_ring(0)
            out.begin_ring(1)
    dk_t = rotate_back(dk_acc[...].T, slice(0, GROUP))
    dqkv_t[4] = dk_t.astype(bf16)
    dqkv[:, :, 512:640] = dk_t.T.astype(bf16).reshape(8, ROWS, HD)
    dqkv_t[5] = dv_acc[...].T.astype(bf16)
    dqkv[:, :, 640:768] = dv_acc[...].astype(bf16).reshape(8, ROWS, HD)
    out.relay_ring(0)
    out.relay_ring(1)

    for step in hidden_steps.values():
        step()
    for copy in inv_copies:
        copy.wait_recv()
    for copy in weight_copies:
        copy.wait()

    def tile_copy(n, slot):
        columns = pl.ds(pl.multiple_of(n * TILE, TILE), TILE)
        return pltpu.make_async_copy(hidden_full.at[:, :, columns], tiles.at[:, :, pl.ds(pl.multiple_of(slot * TILE, TILE), TILE)], tile_sem.at[slot])

    order = (0, 1, 3, 2)
    tile_copy(4 * order[0], 0).start()
    for g, p in enumerate(order):
        following = order[g + 1] if g < 3 else None

        def tile(i, carry, p=p, following=following):
            n = 4 * p + i
            slot = lax.rem(i, 2)
            if following is None:
                @pl.when(i < 3)
                def _():
                    tile_copy(n + 1, 1 - slot).start()
            else:
                tile_copy(n + 1 + lax.div(i + 1, 4) * (4 * (following - p) - 4), 1 - slot).start()
            tile_copy(n, slot).wait()
            columns = pl.ds(pl.multiple_of(n * TILE, TILE), TILE)
            inv = inv_all[...].reshape(GROUP, 128)
            held = tiles[:, :, pl.ds(pl.multiple_of(slot * TILE, TILE), TILE)]
            unit = held.reshape(GROUP, TILE).astype(f32) * jnp.concatenate([inv, inv], axis=1)
            normed = (unit * gain_ref[:, columns]).astype(bf16)
            grads = dqkv[...].reshape(GROUP, 768)
            total = lax.dot_general(grads[:, :256], qkv_part[n, :256, :], NT, preferred_element_type=f32)
            total += lax.dot_general(grads[:, 256:512], qkv_part[n, 256:512, :], NT, preferred_element_type=f32)
            total += lax.dot_general(grads[:, 512:], qkv_part[n, 512:, :], NT, preferred_element_type=f32)
            part[:, :, columns] = total.astype(bf16).reshape(8, ROWS, TILE)
            gain_sum[:, columns] = jnp.sum((total * unit).reshape(ROWS, 8, TILE), axis=0)
            qkv_part[n] = jnp.dot(
                dqkv_t[...].reshape(768, GROUP), normed, preferred_element_type=f32
            ).astype(bf16)
            return carry

        lax.fori_loop(0, 4, tile, 0)
        if p >= tree.over_z:
            tree.begin_z(p)
        else:
            tree.begin_x(1, p)
            tree.begin_x(0, p)
        qkv.core_copy(2 * p).start()
        qkv.core_copy(2 * p + 1).start()
        if g == 1:
            out.send_half()
        if g == 2:
            qkv.begin_ring(0)

    gain_row = jnp.sum(gain_sum[...], axis=0, keepdims=True)
    for i in range(32):
        gain_block[0, i:i + 1, :] = gain_row[:, i * 128:(i + 1) * 128]
    gain_tensor[t] = gain_block[0]
    gain_copies = push_all(tensor_peers, gain_block.at[0], gain_tensor.at[t], gain_t_send, gain_t_recv)

    tree.relay(1, 0)
    tree.relay(0, 0)
    qkv.begin_ring(1)
    tree.relay(1, 1)
    tree.relay(0, 1)
    qkv.relay_ring(0)

    for copy in gain_copies:
        copy.wait_recv()
    gain_total = gain_tensor[0]
    for k in range(1, N_TENSOR):
        gain_total = gain_total + gain_tensor[k]
    gain_block[1] = gain_total
    gain_dp[d] = gain_total
    dp_copies = push_all(dp_peers, gain_block.at[1], gain_dp.at[d], gain_d_send, gain_d_recv)

    tree.z_done(2, 3)
    tree.z_done(3, 3)
    tree.begin_x(0, 3)
    qkv.relay_ring(1)
    tree.root_other(0)
    tree.relay(1, 2)
    tree.relay(0, 2)
    tree.z_done(1, 3)
    tree.root_other(1)
    tree.relay(0, 3)
    qkv.send_half()
    tree.z_done(0, 3)
    tree.root_other(2)
    for b, value in enumerate(out.result()):
        gout_ref[b * 256:(b + 1) * 256, :] = value

    for copy in dp_copies:
        copy.wait_recv()
    gain_total = gain_dp[0]
    for k in range(1, N_DP):
        gain_total = gain_total + gain_dp[k]
    ggain_ref[...] = gain_total

    for copy in loads[-4:]:
        copy.wait()
    inv = inv_own[:, 0:1]
    dots = jnp.zeros((ROWS, 1), f32)
    for p in (0, 1, 3, 2):
        columns = slice(p * STRIPE, (p + 1) * STRIPE)
        scaled = tree.result(p) * gain_ref[:, columns]
        dh_ref[:, columns] = scaled
        unit = kept_hidden[p].astype(f32) * inv
        dots = dots + jnp.sum(scaled * unit, axis=1, keepdims=True)
    mean = dots * (1.0 / D)
    for p in range(4):
        columns = slice(p * STRIPE, (p + 1) * STRIPE)
        unit = kept_hidden[p].astype(f32) * inv
        dh_ref[:, columns] = inv * (dh_ref[:, columns] - unit * mean)
    top, bottom = qkv.result()
    gq_ref[:, :384] = top.T
    gq_ref[:, 384:] = bottom[:128].T
    gk_ref[...] = bottom[128:256].T
    gv_ref[...] = bottom[256:].T

    hidden_tree.finish()
    tree.finish()
    out.finish()
    qkv.finish()
    for copy in source_copies + inv_copies + gain_copies + dp_copies:
        copy.wait_send()


def hand_over(*refs):
    sources, results, held, sems = refs[:6], refs[6:12], refs[12:18], refs[18]
    loads = [pltpu.make_async_copy(sources[i], held[i], sems.at[0, i]) for i in range(6)]
    stores = [pltpu.make_async_copy(held[i], results[i], sems.at[1, i]) for i in range(6)]
    for copy in loads:
        copy.start()
    for before, after in zip(loads, stores):
        before.wait()
        after.start()
    for copy in stores:
        copy.wait()


def per_device(
    hidden_in, teacher, row_source, segments, branch, queries, key_rot, value_rows, attended, norm_gain,
    w_query, w_key, w_value, w_out,
):
    any_space = pl.BlockSpec(memory_space=pl.ANY)
    vmem = pl.BlockSpec(memory_space=pltpu.VMEM)
    dma = pltpu.SemaphoreType.DMA
    scratch = pltpu.VMEM
    stage_sems = [dma((8,)), dma((8,)), dma((2, 6)), dma((2, 6)), dma((1,)), dma((1,))]
    shape = jax.ShapeDtypeStruct
    *results, _ = pl.pallas_call(
        kernel,
        out_shape=(
            shape((ROWS, D), f32), shape((256, 512), f32), shape((256, 128), f32), shape((256, 128), f32),
            shape((512, 256), f32), shape((32, 128), f32), shape((N_TENSOR, ROWS, D), bf16),
        ),
        in_specs=[vmem] * 3 + [any_space] * 11,
        out_specs=(vmem,) * 6 + (any_space,),
        scratch_shapes=[
            scratch((8, ROWS, D), bf16), scratch((8, ROWS, D), bf16), scratch((28, ROWS, STRIPE), bf16),
            scratch((16, 768, 256), bf16), scratch((8, 768, 256), bf16), scratch((2, 6, 384, 256), bf16), scratch((768, 256), bf16),
            scratch((16, 512, 256), bf16), scratch((8, 512, 256), bf16), scratch((2, 6, 256, 256), bf16), scratch((512, 256), bf16),
            scratch((2, 512, 512), bf16), scratch((8, ROWS, 512), bf16),
            scratch((GROUP, 512), bf16), scratch((GROUP, HD), bf16), scratch((GROUP, HD), bf16),
            scratch((HD // 2, GROUP), f32), scratch((HD // 2, GROUP), f32), scratch((GROUP, 128), f32),
            scratch((ROWS, 128), f32), scratch((N_TENSOR, ROWS, 128), f32),
            scratch((GROUP, HD), f32), scratch((GROUP, HD), f32),
            scratch((8, ROWS), jnp.int32), scratch((N_DP, 8, ROWS), jnp.int32),
            scratch((8, D), f32), scratch((2, 32, 128), f32), scratch((N_TENSOR, 32, 128), f32), scratch((N_DP, 32, 128), f32),
            dma((15,)), dma((15,)), dma((15,)), dma((15,)),
            dma((28,)), dma((8, 4)), dma((28,)), dma((8, 4)),
            dma((7,)), dma((7,)), dma((28,)), dma((28,)),
        ] + stage_sems + stage_sems + [
            dma((7,)), dma((7,)), dma((15,)), dma((15,)), dma((40,)), dma((16, 4)), dma((2,)),
        ],
        compiler_params=pltpu.CompilerParams(
            collective_id=1, has_side_effects=True, vmem_limit_bytes=60 * 2**20
        ),
        cost_estimate=pl.CostEstimate(flops=27 * 10**9, bytes_accessed=60 * 2**20, transcendentals=4 * 2**20),
    )(
        row_source[None, :], segments, norm_gain[None, :], teacher, branch, hidden_in, queries, key_rot, value_rows,
        attended, w_query, w_key, w_value, w_out,
    )
    d_hidden, grad_query, grad_key, grad_value, grad_out, grad_gain = pl.pallas_call(
        hand_over,
        out_shape=[shape(value.shape, value.dtype) for value in results],
        in_specs=[any_space] * 6,
        out_specs=[any_space] * 6,
        scratch_shapes=[scratch(value.shape, value.dtype) for value in results] + [dma((2, 6))],
        compiler_params=pltpu.CompilerParams(vmem_limit_bytes=16 * 2**20),
    )(*results)
    return (grad_query, grad_key, grad_value, grad_out, grad_gain.reshape(D), d_hidden)


def solution(mesh):
    return jax.shard_map(
        per_device,
        mesh=mesh,
        in_specs=(
            P(("dp", "tensor"), None),
            P(("dp", "tensor"), None),
            P(("dp", "tensor")),
            P("dp", None),
            P(("dp", "tensor"), None),
            P("dp", "tensor"),
            P("dp", "tensor"),
            P("dp", "tensor"),
            P("dp", "tensor"),
            P(),
            P(None, "tensor"),
            P(None, "tensor"),
            P(None, "tensor"),
            P("tensor", None),
        ),
        out_specs=(
            P("dp", "tensor"),
            P("dp", "tensor"),
            P("dp", "tensor"),
            P("tensor", "dp"),
            P(),
            P(("dp", "tensor"), None),
        ),
        check_vma=False,
    )
```

```python
import jax
import jax.numpy as jnp
import numpy as np
from jax import lax
from jax.experimental import pallas as pl
from jax.experimental.pallas import tpu as pltpu
from jax.sharding import PartitionSpec as P

HEADS = 32
KVH = 8
HD = 128
D = 4096
ROWS = 128
GROUP = 1024
N_DP = 16
N_TENSOR = 8
CAPACITY = 9
CHUNK = 512
SLOTS = 80
PIECE = 32
STRIPE = 1024
TILE = 256

MESH = pl.DeviceIdType.MESH
f32 = jnp.float32
bf16 = jnp.bfloat16
NT = (((1,), (1,)), ((), ()))

theta_base = 500000.0
eps_norm = 1e-05


def place():
    d, t = lax.axis_index("dp"), lax.axis_index("tensor")
    return d, t, lax.div(t, 2), lax.rem(t, 2)


def tensor_index(x, z):
    return x * 2 + z


def greet(ids):
    barrier = pltpu.get_barrier_semaphore()
    for device in ids:
        pl.semaphore_signal(barrier, inc=1, device_id=device, device_id_type=MESH)
    pl.semaphore_wait(barrier, len(ids))


def remote(src, dst, send_sem, recv_sem, to):
    return pltpu.make_async_remote_copy(
        src_ref=src, dst_ref=dst, send_sem=send_sem, recv_sem=recv_sem, device_id=to, device_id_type=MESH
    )


class TreeGather:
    def __init__(self, own, full, send, recv, over_z):
        self.over_z = over_z
        self.own, self.full, self.send_sems, self.recv_sems = own, full, send, recv
        self.d, self.t, self.x, self.z = place()
        self.copies = []
        d, x, z = self.d, self.x, self.z
        right, left, across, other = lax.rem(x + 1, 4), lax.rem(x + 3, 4), lax.rem(x + 2, 4), 1 - z
        self.to_right = (d, tensor_index(right, z))
        self.to_left = (d, tensor_index(left, z))
        self.to_z = (d, tensor_index(x, other))
        self.near = [tensor_index(x, other), tensor_index(left, z), tensor_index(right, z), tensor_index(across, z)]
        self.far = [tensor_index(left, other), tensor_index(right, other), tensor_index(across, other)]

    def piece(self, s, p):
        return self.full.at[s, pl.ds(p * PIECE, PIECE)]

    def send(self, s, p, to, own=False):
        src = self.own.at[pl.ds(p * PIECE, PIECE)] if own else self.piece(s, p)
        copy = remote(src, self.piece(s, p), self.send_sems.at[len(self.copies)], self.recv_sems.at[s, p], to)
        copy.start()
        self.copies.append(copy)

    def wait(self, s, p):
        piece = self.piece(s, p)
        remote(piece, piece, self.send_sems.at[0], self.recv_sems.at[s, p], self.to_z).wait_recv()

    def begin(self):
        by_z = list(range(4))
        by_x = list(range(self.over_z, 4)) + list(range(self.over_z))
        for i in (0, 2):
            a, b = by_x[i:i + 2]
            for p, to in (
                (by_z[i], self.to_z), (a, self.to_right), (b, self.to_left), (by_z[i + 1], self.to_z),
                (b, self.to_right), (a, self.to_left),
            ):
                if to is not self.to_z or p < self.over_z or self.over_z < 4:
                    self.send(self.t, p, to, self.own is not None)

    def steps(self):
        partner, left, right, across = self.near
        far_left, far_right, far_across = self.far
        first = list(range(self.over_z))
        last = list(range(self.over_z, 4))
        order = [(partner, p) for p in first[:2]] + [(s, p) for p in (last + first)[:2] for s in (left, right)]
        order += [(partner, p) for p in first[2:]] + [(s, p) for p in (last + first)[2:] for s in (left, right)]
        order += [(s, p) for p in first for s in (far_left, far_right)] + [(across, p) for p in last + first]
        order += [(far_across, p) for p in first]
        order += [(s, p) for s in (partner, far_left, far_right, far_across) for p in last]

        def targets_of(s, p):
            targets = []
            if s is partner and p < self.over_z:
                targets += [self.to_right, self.to_left]
            if s is left and p % 2 == 0 or s is far_left and p % 2 == 0 and p < self.over_z:
                targets.append(self.to_right)
            if s is right and p % 2 == 1 or s is far_right and p % 2 == 1 and p < self.over_z:
                targets.append(self.to_left)
            if p >= self.over_z and (s is left or s is right or s is across):
                targets.append(self.to_z)
            return targets

        plan = [(s, p, targets_of(s, p)) for s, p in order]

        def make(s, p, targets):
            def step():
                self.wait(s, p)
                for to in targets:
                    self.send(s, p, to)
            return step

        roles = {id(s): name for s, name in (
            (partner, "partner"), (left, "left"), (right, "right"), (across, "across"),
            (far_left, "far_left"), (far_right, "far_right"), (far_across, "far_across"),
        )}
        return {(roles[id(s)], p): make(s, p, targets) for s, p, targets in plan}

    def finish(self):
        for copy in self.copies:
            copy.wait_send()


class TreeScatter:
    def __init__(self, part, slots, send, recv, over_z):
        self.over_z = over_z
        first, last = range(over_z), range(over_z, 4)
        self.part, self.slots, self.send_sems, self.recv_sems = part, slots, send, recv
        self.d, self.t, self.x, self.z = place()
        d, x, z = self.d, self.x, self.z
        self.to_right = (d, tensor_index(lax.rem(x + 1, 4), z))
        self.to_left = (d, tensor_index(lax.rem(x + 3, 4), z))
        self.to_z = (d, tensor_index(x, 1 - z))
        names = [(kind, e, p) for e in (0, 1) for p in first for kind in ("relay", "right", "left")]
        names += [("z", 0, p) for p in first]
        names += [("zz", k, p) for k in range(4) for p in last]
        names += [(kind, 0, p) for p in last for kind in ("relay", "right", "left")]
        self.index = {name: n for n, name in enumerate(names)}
        self.copies = []

    def dest(self, k, e):
        z = self.z if e == 0 else 1 - self.z
        return tensor_index(lax.rem(self.x + k, 4), z)

    def stripe(self, p):
        return pl.ds(p * STRIPE, STRIPE)

    def send(self, k, e, p, to, name):
        n = self.index[name]
        copy = remote(
            self.part.at[self.dest(k, e), :, self.stripe(p)], self.slots.at[n], self.send_sems.at[len(self.copies)],
            self.recv_sems.at[n], to,
        )
        copy.start()
        self.copies.append(copy)

    def wait(self, name):
        n = self.index[name]
        slot = self.slots.at[n]
        remote(slot, slot, self.send_sems.at[0], self.recv_sems.at[n], self.to_z).wait_recv()

    def total(self, k, e, p, names):
        for name in names:
            self.wait(name)
        total = self.part[self.dest(k, e), :, self.stripe(p)].astype(f32)
        for name in names:
            total = total + self.slots[self.index[name]].astype(f32)
        return total

    def add(self, k, e, p, names):
        self.part[self.dest(k, e), :, self.stripe(p)] = self.total(k, e, p, names).astype(bf16)

    def begin_z(self, p):
        for k in (2, 1, 3, 0):
            self.send(k, 1, p, self.to_z, ("zz", k, p))

    def begin_x(self, e, p):
        if p % 2 == 0:
            self.send(2, e, p, self.to_left, ("relay", e, p))
            self.send(1, e, p, self.to_right, ("left", e, p))
        else:
            self.send(2, e, p, self.to_right, ("relay", e, p))
            self.send(3, e, p, self.to_left, ("right", e, p))

    def relay(self, e, p):
        if p % 2 == 0:
            self.add(3, e, p, [("relay", e, p)])
            self.send(3, e, p, self.to_left, ("right", e, p))
        else:
            self.add(1, e, p, [("relay", e, p)])
            self.send(1, e, p, self.to_right, ("left", e, p))

    def z_done(self, k, p):
        self.add(k, 0, p, [("zz", k, p)])

    def root_other(self, p):
        self.add(0, 1, p, [("right", 1, p), ("left", 1, p)])
        self.send(0, 1, p, self.to_z, ("z", 0, p))

    def result(self, p):
        names = [("right", 0, p), ("left", 0, p)]
        return self.total(0, 0, p, names + [("z", 0, p)] if p < self.over_z else names)

    def finish(self):
        for copy in self.copies:
            copy.wait_send()


class StageScatter:
    def __init__(self, part, core, ring, half, sems):
        self.part, self.core, self.ring, self.half = part, core, ring, half
        self.core_send, self.core_recv, self.ring_send, self.ring_recv, self.half_send, self.half_recv = sems
        d, t, _, _ = place()
        self.c, self.y, self.zh = lax.rem(d, 2), lax.rem(lax.div(d, 2), 4), lax.div(d, 8)
        self.to_core = (d + 1 - 2 * self.c, t)
        self.to_right = ((self.zh * 4 + lax.rem(self.y + 1, 4)) * 2 + self.c, t)
        self.to_left = ((self.zh * 4 + lax.rem(self.y + 3, 4)) * 2 + self.c, t)
        self.to_half = (((1 - self.zh) * 4 + self.y) * 2 + self.c, t)
        self.cut = core.shape[1] // 2
        self.copies = []

    def core_copy(self, j):
        return remote(
            self.part.at[2 * j + 1 - self.c], self.core.at[j], self.core_send.at[j], self.core_recv.at[j], self.to_core
        )

    def block(self, k, half):
        return 2 * (half * 4 + lax.rem(self.y + k, 4)) + self.c

    def fold_core(self, k, half):
        n = self.block(k, half)
        j = lax.div(n, 2)
        self.core_copy(j).wait_recv()
        self.part[n] = (self.part[n].astype(f32) + self.core[j].astype(f32)).astype(bf16)

    def rows(self, b):
        return pl.ds(b * self.cut, self.cut)

    def send(self, k, half, b, to, slot):
        copy = remote(
            self.part.at[self.block(k, half), self.rows(b)], self.ring.at[half, slot],
            self.ring_send.at[half, slot], self.ring_recv.at[half, slot], to,
        )
        copy.start()
        self.copies.append(copy)

    def wait(self, half, slot):
        ref = self.ring.at[half, slot]
        remote(ref, ref, self.ring_send.at[half, slot], self.ring_recv.at[half, slot], self.to_core).wait_recv()

    def begin_ring(self, half):
        self.fold_core(2, half)
        self.send(2, half, 0, self.to_left, 0)
        self.send(2, half, 1, self.to_right, 1)
        self.fold_core(1, half)
        self.send(1, half, 0, self.to_right, 2)
        self.fold_core(3, half)
        self.send(3, half, 1, self.to_left, 5)
        self.fold_core(0, half)

    def relay_ring(self, half):
        for k, b, slot, to, target in ((3, 0, 0, self.to_left, 4), (1, 1, 1, self.to_right, 3)):
            self.wait(half, slot)
            n = self.block(k, half)
            total = self.part[n, self.rows(b)].astype(f32) + self.ring[half, slot].astype(f32)
            self.part[n, self.rows(b)] = total.astype(bf16)
            self.send(k, half, b, to, target)

    def ring_total(self, half, b):
        total = self.part[self.block(0, half), self.rows(b)].astype(f32)
        for slot in (2 + b, 4 + b):
            self.wait(half, slot)
            total = total + self.ring[half, slot].astype(f32)
        return total

    def send_half(self):
        n = self.block(0, 1 - self.zh)
        for b in (0, 1):
            self.part[n, self.rows(b)] = self.ring_total(1 - self.zh, b).astype(bf16)
        copy = remote(self.part.at[n], self.half, self.half_send, self.half_recv, self.to_half)
        copy.start()
        self.half_copy = copy

    def result(self):
        totals = [self.ring_total(self.zh, b) for b in (0, 1)]
        self.half_copy.wait_recv()
        return [total + self.half[self.rows(b), :].astype(f32) for b, total in enumerate(totals)]

    def finish(self):
        for copy in self.copies:
            copy.wait_send()
        self.half_copy.wait_send()
        for j in range(8):
            self.core_copy(j).wait_send()


def kernel(
    source_ref, seg_ref, gain_ref, teacher_ref, branch_ref, hidden_ref, q_in, k_in, v_in, att_in, wq_in, wk_in,
    wv_in, w_out_in,
    dh_ref, gq_ref, gk_ref, gv_ref, gout_ref, ggain_ref, hidden_full,
    part, slope, slots, qkv_part, qkv_core, qkv_ring, qkv_half, out_part, out_core, out_ring, out_half,
    att_t, d_att, q_ref, k_ref, v_ref, cos_ref, sin_ref, seg_col, inv_own, inv_all, dk_acc, dv_acc,
    request, sources, gain_sum, gain_block, gain_tensor, gain_dp,
    source_send, source_recv, parcel_send, parcel_recv, hidden_send, hidden_recv, slope_send, slope_recv,
    inv_send, inv_recv, part_send, part_recv,
    qkv_core_send, qkv_core_recv, qkv_ring_send, qkv_ring_recv, qkv_half_send, qkv_half_recv,
    out_core_send, out_core_recv, out_ring_send, out_ring_recv, out_half_send, out_half_recv,
    gain_t_send, gain_t_recv, gain_d_send, gain_d_recv, load_sem, weight_sem, tile_sem,
):
    d, t, x, z = place()
    teacher, branch, own_hidden = part.at[0], part.at[1], part.at[2]
    dqkv = slope.at[:, :, pl.ds(0, 768)]
    dqkv_t = slope.at[pl.ds(0, 6), :, pl.ds(1024, 1024)]
    kept_hidden = slope.at[pl.ds(0, 4), :, pl.ds(2048, STRIPE)]
    tiles = slope.at[:, :, pl.ds(3072, 512)]

    loads = []

    def load(src, dst):
        copy = pltpu.make_async_copy(src, dst, load_sem.at[len(loads)])
        copy.start()
        loads.append(copy)
        return copy

    load_hidden = load(hidden_ref, own_hidden)
    load_teacher = load(teacher_ref, teacher)
    load_branch = load(branch_ref, branch)

    tensor_peers = [(d, lax.rem(t + k, N_TENSOR)) for k in range(1, N_TENSOR)]
    dp_peers = [(lax.rem(d + k, N_DP), t) for k in range(1, N_DP)]
    hidden_tree = TreeGather(hidden_ref, hidden_full, hidden_send, hidden_recv, 3)
    slope_tree = TreeGather(None, slope, slope_send, slope_recv, 2)
    tree = TreeScatter(part, slots, part_send, part_recv, 3)
    qkv = StageScatter(
        qkv_part, qkv_core, qkv_ring, qkv_half,
        (qkv_core_send, qkv_core_recv, qkv_ring_send, qkv_ring_recv, qkv_half_send.at[0], qkv_half_recv.at[0]),
    )
    out = StageScatter(
        out_part, out_core, out_ring, out_half,
        (out_core_send, out_core_recv, out_ring_send, out_ring_recv, out_half_send.at[0], out_half_recv.at[0]),
    )
    request[...] = jnp.broadcast_to(source_ref[...], (8, ROWS))
    greet(tensor_peers + dp_peers)

    def push_all(peers, src, dst, send, recv):
        copies = [remote(src, dst, send.at[k], recv.at[k], to) for k, to in enumerate(peers)]
        for copy in copies:
            copy.start()
        return copies

    source_copies = push_all(dp_peers, request, sources.at[d], source_send, source_recv)
    hidden_tree.begin()
    sources[d] = request[...]
    load_att = [load(att_in.at[pl.ds(s * ROWS, ROWS)], d_att.at[s]) for s in range(8)]
    load_w_out = [
        load(w_out_in.at[:, pl.ds(n * TILE, TILE)], qkv_part.at[n, pl.ds(0, 512)]) for n in range(16)
    ]
    load_qkv = [load(q_in, q_ref), load(k_in, k_ref), load(v_in, v_ref)]

    above = (
        lax.broadcasted_iota(jnp.int32, (ROWS, ROWS), 0) < lax.broadcasted_iota(jnp.int32, (ROWS, ROWS), 1)
    ).astype(bf16)
    block_row = lax.broadcasted_iota(jnp.int32, (SLOTS, ROWS), 0)
    chunk_ids = lax.shift_right_logical(block_row * 57, 9)
    slot_ids = block_row - CAPACITY * chunk_ids
    peer_ids = lax.broadcasted_iota(jnp.int32, (N_DP, ROWS), 0)
    row_ids = lax.broadcasted_iota(jnp.int32, (ROWS, ROWS), 0)

    def slot_onehot(mask, rank, q):
        return ((slot_ids == rank[q:q + 1]) & (mask[q:q + 1] > 0)).astype(f32).astype(bf16)

    def ranks(mask):
        return jnp.dot(mask.astype(bf16), above, preferred_element_type=f32).astype(jnp.int32)

    from_peer = (peer_ids == lax.shift_right_logical(source_ref[...], 10)).astype(f32)
    taken = jnp.sum(from_peer * (SLOTS * peer_ids + ranks(from_peer)).astype(f32), axis=0, keepdims=True)
    taken = jnp.concatenate([jnp.broadcast_to(taken, (ROWS, ROWS)).T] * 10, axis=1)
    lanes = lax.broadcasted_iota(jnp.int32, (ROWS, N_DP * SLOTS), 1).astype(f32)
    for k in range(8):
        onehot = (lanes == taken + CAPACITY * k).astype(f32).astype(bf16)
        for n in range(5):
            out_part[2 * n + k // 4, (k % 4) * ROWS:(k % 4 + 1) * ROWS, :] = onehot[:, n * TILE:(n + 1) * TILE]

    for copy in source_copies:
        copy.wait_recv()
    wanted = jnp.concatenate([sources[q, 0:1, :] for q in range(N_DP)], axis=0)
    mine = (lax.shift_right_logical(wanted, 10) == d).astype(f32)
    rank = ranks(mine)
    local_row = jnp.bitwise_and(wanted, ROWS - 1)
    picks = []
    for q in range(N_DP):
        row_onehot = (row_ids == local_row[q:q + 1]).astype(f32).astype(bf16)
        picks.append(lax.dot_general(slot_onehot(mine, rank, q), row_onehot, NT, preferred_element_type=f32))
    load_teacher.wait()
    chunks = jnp.concatenate([teacher[:, k * CHUNK:(k + 1) * CHUNK] for k in range(8)], axis=0)
    for b in range(4):
        pick = jnp.concatenate([
            jnp.concatenate([jnp.where(chunk_ids == k, picks[q], 0.0).astype(bf16) for k in range(8)], axis=1)
            for q in range(4 * b, 4 * b + 4)
        ], axis=0)
        values = jnp.dot(pick, chunks, preferred_element_type=f32).astype(bf16)
        for i in range(4):
            q = 4 * b + i
            part[3 + q // 8, :SLOTS, (q % 8) * CHUNK:(q % 8 + 1) * CHUNK] = values[i * SLOTS:(i + 1) * SLOTS]

    def slot_rows(first, q):
        columns = pl.ds(pl.multiple_of(lax.rem(q, 8) * CHUNK, CHUNK), CHUNK)
        return part.at[first + lax.div(q, 8), pl.ds(0, SLOTS), columns]

    parcel_copies = []
    for k, to in enumerate(dp_peers):
        copy = remote(slot_rows(3, to[0]), slot_rows(5, d), parcel_send.at[k], parcel_recv.at[k], to)
        copy.start()
        parcel_copies.append(copy)
    keep_own = load(slot_rows(3, d), slot_rows(5, d))

    load_hidden.wait()
    load_kept = load(own_hidden, hidden_full.at[t])
    squares = jnp.zeros((ROWS, 128), f32)
    for n in range(0, D, 128):
        values = own_hidden[:, n:n + 128].astype(f32)
        squares = squares + values * values
    inv_rms = lax.rsqrt(jnp.sum(squares, axis=1, keepdims=True) * (1.0 / D) + eps_norm)
    inv_own[...] = jnp.broadcast_to(inv_rms, (ROWS, 128))
    inv_copies = push_all(tensor_peers, inv_own, inv_all.at[t], inv_send, inv_recv)
    inv_all[t] = inv_own[...]

    hidden_steps = hidden_tree.steps()
    slope_steps = slope_tree.steps()

    def take(steps, *names):
        for role, p in names:
            steps.pop((role, p))()

    take(hidden_steps, ("partner", 0), ("left", 3), ("right", 3), ("left", 0))

    seg_row = seg_ref[...].astype(f32)
    before = jnp.zeros_like(seg_row)
    for value in range(3):
        count = jnp.sum((seg_row == value).astype(f32), axis=1, keepdims=True)
        before = before + jnp.where(seg_row > value, count, 0.0)
    positions = lax.broadcasted_iota(jnp.int32, (1, GROUP), 1).astype(f32) - before
    steps_down = lax.broadcasted_iota(jnp.int32, (HD // 2, 128), 0).astype(f32)
    frequency = jnp.exp(steps_down * float(-2.0 * np.log(theta_base) / HD))
    for n in range(0, GROUP, 128):
        angles = frequency * positions[:, n:n + 128]
        cos_ref[:, n:n + 128] = jnp.cos(angles)
        sin_ref[:, n:n + 128] = jnp.sin(angles)
    seg_col[...] = jnp.broadcast_to(seg_row, (128, GROUP)).T

    take(hidden_steps, ("partner", 1), ("right", 1))
    for copy in load_att:
        copy.wait()
    for e in (0, 1):
        rows = jnp.concatenate([d_att[2 * i + e] for i in range(4)], axis=0)
        att_t[e] = rows.astype(f32).T.astype(bf16)
    take(hidden_steps, ("left", 2))

    keep_own.wait()
    load_branch.wait()
    for copy in parcel_copies:
        copy.wait_recv()
    came = jnp.concatenate(
        [part[5 + q // 8, :SLOTS, (q % 8) * CHUNK:(q % 8 + 1) * CHUNK] for q in range(N_DP)], axis=0
    )
    for b in (0, 1):
        onehot = jnp.concatenate([out_part[2 * n + b] for n in range(5)], axis=1)
        target = jnp.dot(onehot, came, preferred_element_type=f32)
        for i in range(4):
            columns = slice((4 * b + i) * CHUNK, (4 * b + i + 1) * CHUNK)
            change = branch[:, columns].astype(f32) - target[i * ROWS:(i + 1) * ROWS]
            slope[t, :, columns] = (change * (N_DP * GROUP) ** -0.5).astype(bf16)
    slope_tree.begin()
    for copy in parcel_copies:
        copy.wait_send()

    for copy in load_qkv:
        copy.wait()
    blk = 256
    scale = HD ** -0.5

    def forward(i):
        rows = slice(i * blk, (i + 1) * blk)
        seen = (i + 1) * blk
        keys = jnp.concatenate([seg_col[:seen, :]] * 2, axis=1)
        allowed = (keys == seg_row[:, rows]) & (
            lax.broadcasted_iota(jnp.int32, (seen, blk), 0) <= lax.broadcasted_iota(jnp.int32, (seen, blk), 1) + i * blk
        )
        for h in range(4):
            scores = lax.dot_general(
                k_ref[:seen, :], q_ref[rows, h * HD:(h + 1) * HD], NT, preferred_element_type=f32
            ) * scale
            scores = jnp.where(allowed, scores, -1e30)
            weights = jnp.where(allowed, jnp.exp(scores - jnp.max(scores, axis=0, keepdims=True)), 0.0)
            soft = (weights * (1.0 / jnp.sum(weights, axis=0, keepdims=True))).astype(bf16)
            first = (4 * i + h) * blk
            part[:2 * (i + 1), :, first:first + blk] = soft.reshape(2 * (i + 1), ROWS, blk)

    load_kept.wait()
    take(hidden_steps, ("far_left", 0), ("far_right", 1), ("across", 3))
    forward(0)
    take(slope_steps, ("partner", 0), ("partner", 1))
    forward(1)
    take(slope_steps, ("left", 2), ("right", 3), ("left", 3), ("right", 2))
    forward(2)
    take(slope_steps, ("left", 0), ("right", 1))
    take(hidden_steps, ("partner", 2))
    take(slope_steps, ("far_left", 0), ("far_right", 1))
    forward(3)

    for p in (2, 3, 0, 1):
        take(slope_steps, ("across", p))
    take(slope_steps, ("left", 1), ("right", 0))
    for copy in load_w_out:
        copy.wait()

    def slope_rows(e, columns):
        return jnp.concatenate([slope[2 * i + e, :, columns] for i in range(4)], axis=0)

    def attended_slope(e):
        def tile(n, carry):
            heads = pl.ds(pl.multiple_of(n * 256, 256), 256)
            value = jnp.zeros((512, 256), f32)
            for k in range(16):
                rows = slope_rows(e, slice(k * TILE, (k + 1) * TILE))
                value += lax.dot_general(rows, qkv_part[k, heads, :], NT, preferred_element_type=f32)
            value = value.astype(bf16)
            for i in range(4):
                d_att[2 * i + e, :, heads] = value[i * ROWS:(i + 1) * ROWS]
            return carry

        lax.fori_loop(0, 2, tile, 0)

    def out_gradient(e, first):
        def tile(n, carry):
            columns = pl.ds(pl.multiple_of(n * TILE, TILE), TILE)
            value = jnp.dot(att_t[e], slope_rows(e, columns), preferred_element_type=f32)
            if not first:
                value = value + out_part[n].astype(f32)
            out_part[n] = value.astype(bf16)
            return carry

        return tile

    attended_slope(z)
    lax.fori_loop(0, 16, out_gradient(z, True), 0)
    take(hidden_steps, ("far_left", 2))
    for step in slope_steps.values():
        step()
    attended_slope(1 - z)
    weight_copies = []
    for n in range(16):
        rows = pl.ds(n * TILE, TILE)
        for i, (src, dst) in enumerate((
            (wq_in.at[rows, pl.ds(0, 256)], qkv_part.at[n, pl.ds(0, 256)]),
            (wq_in.at[rows, pl.ds(256, 256)], qkv_part.at[n, pl.ds(256, 256)]),
            (wk_in.at[rows], qkv_part.at[n, pl.ds(512, 256), pl.ds(0, 128)]),
            (wv_in.at[rows], qkv_part.at[n, pl.ds(512, 256), pl.ds(128, 128)]),
        )):
            copy = pltpu.make_async_copy(src, dst, weight_sem.at[n, i])
            copy.start()
            weight_copies.append(copy)
    slope_tree.finish()
    lax.fori_loop(0, 16, out_gradient(1 - z, False), 0)
    for j in range(8):
        out.core_copy(j).start()
    for p in range(4):
        load(hidden_ref.at[:, pl.ds(p * STRIPE, STRIPE)], kept_hidden.at[p])

    dk_acc[...] = jnp.zeros_like(dk_acc)
    dv_acc[...] = jnp.zeros_like(dv_acc)
    k_t = k_ref[...].astype(f32).T.astype(bf16)

    def rotate_back(values, columns):
        u, w = values[:64], values[64:]
        c, s = cos_ref[:, columns], sin_ref[:, columns]
        return jnp.concatenate([u * c + w * s, w * c - u * s], axis=0)

    for i in range(GROUP // blk):
        rows = slice(i * blk, (i + 1) * blk)
        seen = (i + 1) * blk
        for h in range(4):
            cols = slice(h * HD, (h + 1) * HD)
            q = q_ref[rows, cols]
            da = d_att[2 * i:2 * i + 2, :, cols].reshape(blk, HD)
            first = (4 * i + h) * blk
            probs = part[:2 * (i + 1), :, first:first + blk].reshape(seen, blk)
            soft = probs.astype(f32)
            d_probs = lax.dot_general(v_ref[:seen, :], da, NT, preferred_element_type=f32)
            delta = jnp.sum(soft * d_probs, axis=0, keepdims=True)
            d_scores = (soft * (d_probs - delta) * scale).astype(bf16)
            dv_acc[:seen, :] += jnp.dot(probs, da, preferred_element_type=f32)
            dk_acc[:seen, :] += jnp.dot(d_scores, q, preferred_element_type=f32)
            dq_t = rotate_back(jnp.dot(k_t[:, :seen], d_scores, preferred_element_type=f32), rows)
            dqkv_t[h, :, rows] = dq_t.astype(bf16)
            dqkv[2 * i:2 * i + 2, :, cols] = dq_t.T.astype(bf16).reshape(2, ROWS, HD)
        if i == 1:
            out.begin_ring(0)
            out.begin_ring(1)
    dk_t = rotate_back(dk_acc[...].T, slice(0, GROUP))
    dqkv_t[4] = dk_t.astype(bf16)
    dqkv[:, :, 512:640] = dk_t.T.astype(bf16).reshape(8, ROWS, HD)
    dqkv_t[5] = dv_acc[...].T.astype(bf16)
    dqkv[:, :, 640:768] = dv_acc[...].astype(bf16).reshape(8, ROWS, HD)
    out.relay_ring(0)
    out.relay_ring(1)

    for step in hidden_steps.values():
        step()
    for copy in inv_copies:
        copy.wait_recv()
    for copy in weight_copies:
        copy.wait()

    def tile_copy(n, slot):
        columns = pl.ds(pl.multiple_of(n * TILE, TILE), TILE)
        return pltpu.make_async_copy(hidden_full.at[:, :, columns], tiles.at[:, :, pl.ds(pl.multiple_of(slot * TILE, TILE), TILE)], tile_sem.at[slot])

    order = (0, 1, 3, 2)
    tile_copy(4 * order[0], 0).start()
    for g, p in enumerate(order):
        following = order[g + 1] if g < 3 else None

        def tile(i, carry, p=p, following=following):
            n = 4 * p + i
            slot = lax.rem(i, 2)
            if following is None:
                @pl.when(i < 3)
                def _():
                    tile_copy(n + 1, 1 - slot).start()
            else:
                tile_copy(n + 1 + lax.div(i + 1, 4) * (4 * (following - p) - 4), 1 - slot).start()
            tile_copy(n, slot).wait()
            columns = pl.ds(pl.multiple_of(n * TILE, TILE), TILE)
            inv = inv_all[...].reshape(GROUP, 128)
            held = tiles[:, :, pl.ds(pl.multiple_of(slot * TILE, TILE), TILE)]
            unit = held.reshape(GROUP, TILE).astype(f32) * jnp.concatenate([inv, inv], axis=1)
            normed = (unit * gain_ref[:, columns]).astype(bf16)
            grads = dqkv[...].reshape(GROUP, 768)
            total = lax.dot_general(grads[:, :256], qkv_part[n, :256, :], NT, preferred_element_type=f32)
            total += lax.dot_general(grads[:, 256:512], qkv_part[n, 256:512, :], NT, preferred_element_type=f32)
            total += lax.dot_general(grads[:, 512:], qkv_part[n, 512:, :], NT, preferred_element_type=f32)
            part[:, :, columns] = total.astype(bf16).reshape(8, ROWS, TILE)
            gain_sum[:, columns] = jnp.sum((total * unit).reshape(ROWS, 8, TILE), axis=0)
            qkv_part[n] = jnp.dot(
                dqkv_t[...].reshape(768, GROUP), normed, preferred_element_type=f32
            ).astype(bf16)
            return carry

        lax.fori_loop(0, 4, tile, 0)
        if p >= tree.over_z:
            tree.begin_z(p)
        else:
            tree.begin_x(1, p)
            tree.begin_x(0, p)
        qkv.core_copy(2 * p).start()
        qkv.core_copy(2 * p + 1).start()
        if g == 1:
            out.send_half()
        if g == 2:
            qkv.begin_ring(0)

    gain_row = jnp.sum(gain_sum[...], axis=0, keepdims=True)
    for i in range(32):
        gain_block[0, i:i + 1, :] = gain_row[:, i * 128:(i + 1) * 128]
    gain_tensor[t] = gain_block[0]
    gain_copies = push_all(tensor_peers, gain_block.at[0], gain_tensor.at[t], gain_t_send, gain_t_recv)

    tree.relay(1, 0)
    tree.relay(0, 0)
    tree.z_done(2, 3)
    qkv.begin_ring(1)
    qkv.relay_ring(0)
    tree.z_done(1, 3)

    for copy in gain_copies:
        copy.wait_recv()
    gain_total = gain_tensor[0]
    for k in range(1, N_TENSOR):
        gain_total = gain_total + gain_tensor[k]
    gain_block[1] = gain_total
    gain_dp[d] = gain_total
    dp_copies = push_all(dp_peers, gain_block.at[1], gain_dp.at[d], gain_d_send, gain_d_recv)

    tree.relay(1, 1)
    tree.relay(0, 1)
    tree.z_done(3, 3)
    tree.begin_x(0, 3)
    qkv.relay_ring(1)
    tree.z_done(0, 3)
    tree.root_other(0)
    qkv.send_half()
    tree.relay(1, 2)
    tree.relay(0, 2)
    tree.root_other(1)
    tree.relay(0, 3)
    tree.root_other(2)
    for b, value in enumerate(out.result()):
        gout_ref[b * 256:(b + 1) * 256, :] = value

    for copy in dp_copies:
        copy.wait_recv()
    gain_total = gain_dp[0]
    for k in range(1, N_DP):
        gain_total = gain_total + gain_dp[k]
    ggain_ref[...] = gain_total

    for copy in loads[-4:]:
        copy.wait()
    inv = inv_own[:, 0:1]
    dots = jnp.zeros((ROWS, 1), f32)
    for p in (0, 1, 3, 2):
        columns = slice(p * STRIPE, (p + 1) * STRIPE)
        scaled = tree.result(p) * gain_ref[:, columns]
        dh_ref[:, columns] = scaled
        unit = kept_hidden[p].astype(f32) * inv
        dots = dots + jnp.sum(scaled * unit, axis=1, keepdims=True)
    mean = dots * (1.0 / D)
    for p in range(4):
        columns = slice(p * STRIPE, (p + 1) * STRIPE)
        unit = kept_hidden[p].astype(f32) * inv
        dh_ref[:, columns] = inv * (dh_ref[:, columns] - unit * mean)
    top, bottom = qkv.result()
    gq_ref[:, :384] = top.T
    gq_ref[:, 384:] = bottom[:128].T
    gk_ref[...] = bottom[128:256].T
    gv_ref[...] = bottom[256:].T

    hidden_tree.finish()
    tree.finish()
    out.finish()
    qkv.finish()
    for copy in source_copies + inv_copies + gain_copies + dp_copies:
        copy.wait_send()


def hand_over(*refs):
    sources, results, held, sems = refs[:6], refs[6:12], refs[12:18], refs[18]
    loads = [pltpu.make_async_copy(sources[i], held[i], sems.at[0, i]) for i in range(6)]
    stores = [pltpu.make_async_copy(held[i], results[i], sems.at[1, i]) for i in range(6)]
    for copy in loads:
        copy.start()
    for before, after in zip(loads, stores):
        before.wait()
        after.start()
    for copy in stores:
        copy.wait()


def per_device(
    hidden_in, teacher, row_source, segments, branch, queries, key_rot, value_rows, attended, norm_gain,
    w_query, w_key, w_value, w_out,
):
    any_space = pl.BlockSpec(memory_space=pl.ANY)
    vmem = pl.BlockSpec(memory_space=pltpu.VMEM)
    dma = pltpu.SemaphoreType.DMA
    scratch = pltpu.VMEM
    stage_sems = [dma((8,)), dma((8,)), dma((2, 6)), dma((2, 6)), dma((1,)), dma((1,))]
    shape = jax.ShapeDtypeStruct
    *results, _ = pl.pallas_call(
        kernel,
        out_shape=(
            shape((ROWS, D), f32), shape((256, 512), f32), shape((256, 128), f32), shape((256, 128), f32),
            shape((512, 256), f32), shape((32, 128), f32), shape((N_TENSOR, ROWS, D), bf16),
        ),
        in_specs=[vmem] * 3 + [any_space] * 11,
        out_specs=(vmem,) * 6 + (any_space,),
        scratch_shapes=[
            scratch((8, ROWS, D), bf16), scratch((8, ROWS, D), bf16), scratch((28, ROWS, STRIPE), bf16),
            scratch((16, 768, 256), bf16), scratch((8, 768, 256), bf16), scratch((2, 6, 384, 256), bf16), scratch((768, 256), bf16),
            scratch((16, 512, 256), bf16), scratch((8, 512, 256), bf16), scratch((2, 6, 256, 256), bf16), scratch((512, 256), bf16),
            scratch((2, 512, 512), bf16), scratch((8, ROWS, 512), bf16),
            scratch((GROUP, 512), bf16), scratch((GROUP, HD), bf16), scratch((GROUP, HD), bf16),
            scratch((HD // 2, GROUP), f32), scratch((HD // 2, GROUP), f32), scratch((GROUP, 128), f32),
            scratch((ROWS, 128), f32), scratch((N_TENSOR, ROWS, 128), f32),
            scratch((GROUP, HD), f32), scratch((GROUP, HD), f32),
            scratch((8, ROWS), jnp.int32), scratch((N_DP, 8, ROWS), jnp.int32),
            scratch((8, D), f32), scratch((2, 32, 128), f32), scratch((N_TENSOR, 32, 128), f32), scratch((N_DP, 32, 128), f32),
            dma((15,)), dma((15,)), dma((15,)), dma((15,)),
            dma((28,)), dma((8, 4)), dma((28,)), dma((8, 4)),
            dma((7,)), dma((7,)), dma((28,)), dma((28,)),
        ] + stage_sems + stage_sems + [
            dma((7,)), dma((7,)), dma((15,)), dma((15,)), dma((40,)), dma((16, 4)), dma((2,)),
        ],
        compiler_params=pltpu.CompilerParams(
            collective_id=1, has_side_effects=True, vmem_limit_bytes=60 * 2**20
        ),
        cost_estimate=pl.CostEstimate(flops=27 * 10**9, bytes_accessed=60 * 2**20, transcendentals=4 * 2**20),
    )(
        row_source[None, :], segments, norm_gain[None, :], teacher, branch, hidden_in, queries, key_rot, value_rows,
        attended, w_query, w_key, w_value, w_out,
    )
    d_hidden, grad_query, grad_key, grad_value, grad_out, grad_gain = pl.pallas_call(
        hand_over,
        out_shape=[shape(value.shape, value.dtype) for value in results],
        in_specs=[any_space] * 6,
        out_specs=[any_space] * 6,
        scratch_shapes=[scratch(value.shape, value.dtype) for value in results] + [dma((2, 6))],
        compiler_params=pltpu.CompilerParams(vmem_limit_bytes=60 * 2**20),
    )(*results)
    return (grad_query, grad_key, grad_value, grad_out, grad_gain.reshape(D), d_hidden)


def solution(mesh):
    return jax.shard_map(
        per_device,
        mesh=mesh,
        in_specs=(
            P(("dp", "tensor"), None),
            P(("dp", "tensor"), None),
            P(("dp", "tensor")),
            P("dp", None),
            P(("dp", "tensor"), None),
            P("dp", "tensor"),
            P("dp", "tensor"),
            P("dp", "tensor"),
            P("dp", "tensor"),
            P(),
            P(None, "tensor"),
            P(None, "tensor"),
            P(None, "tensor"),
            P("tensor", None),
        ),
        out_specs=(
            P("dp", "tensor"),
            P("dp", "tensor"),
            P("dp", "tensor"),
            P("tensor", "dp"),
            P(),
            P(("dp", "tensor"), None),
        ),
        check_vma=False,
    )
```

```python
import jax
import jax.numpy as jnp
import numpy as np
from jax import lax
from jax.experimental import pallas as pl
from jax.experimental.pallas import tpu as pltpu
from jax.sharding import PartitionSpec as P

HEADS = 32
KVH = 8
HD = 128
D = 4096
ROWS = 128
GROUP = 1024
N_DP = 16
N_TENSOR = 8
CAPACITY = 9
CHUNK = 512
SLOTS = 80
PIECE = 32
STRIPE = 1024
TILE = 256

MESH = pl.DeviceIdType.MESH
f32 = jnp.float32
bf16 = jnp.bfloat16
NT = (((1,), (1,)), ((), ()))

theta_base = 500000.0
eps_norm = 1e-05


def place():
    d, t = lax.axis_index("dp"), lax.axis_index("tensor")
    return d, t, lax.div(t, 2), lax.rem(t, 2)


def tensor_index(x, z):
    return x * 2 + z


def greet(ids):
    barrier = pltpu.get_barrier_semaphore()
    for device in ids:
        pl.semaphore_signal(barrier, inc=1, device_id=device, device_id_type=MESH)
    pl.semaphore_wait(barrier, len(ids))


def remote(src, dst, send_sem, recv_sem, to):
    return pltpu.make_async_remote_copy(
        src_ref=src, dst_ref=dst, send_sem=send_sem, recv_sem=recv_sem, device_id=to, device_id_type=MESH
    )


class TreeGather:
    def __init__(self, own, full, send, recv, over_z):
        self.over_z = over_z
        self.own, self.full, self.send_sems, self.recv_sems = own, full, send, recv
        self.d, self.t, self.x, self.z = place()
        self.copies = []
        d, x, z = self.d, self.x, self.z
        right, left, across, other = lax.rem(x + 1, 4), lax.rem(x + 3, 4), lax.rem(x + 2, 4), 1 - z
        self.to_right = (d, tensor_index(right, z))
        self.to_left = (d, tensor_index(left, z))
        self.to_z = (d, tensor_index(x, other))
        self.near = [tensor_index(x, other), tensor_index(left, z), tensor_index(right, z), tensor_index(across, z)]
        self.far = [tensor_index(left, other), tensor_index(right, other), tensor_index(across, other)]

    def piece(self, s, p):
        return self.full.at[s, pl.ds(p * PIECE, PIECE)]

    def send(self, s, p, to, own=False):
        src = self.own.at[pl.ds(p * PIECE, PIECE)] if own else self.piece(s, p)
        copy = remote(src, self.piece(s, p), self.send_sems.at[len(self.copies)], self.recv_sems.at[s, p], to)
        copy.start()
        self.copies.append(copy)

    def wait(self, s, p):
        piece = self.piece(s, p)
        remote(piece, piece, self.send_sems.at[0], self.recv_sems.at[s, p], self.to_z).wait_recv()

    def begin(self):
        by_z = list(range(4))
        by_x = list(range(self.over_z, 4)) + list(range(self.over_z))
        for i in (0, 2):
            a, b = by_x[i:i + 2]
            for p, to in (
                (by_z[i], self.to_z), (a, self.to_right), (b, self.to_left), (by_z[i + 1], self.to_z),
                (b, self.to_right), (a, self.to_left),
            ):
                if to is not self.to_z or p < self.over_z or self.over_z < 4:
                    self.send(self.t, p, to, self.own is not None)

    def steps(self):
        partner, left, right, across = self.near
        far_left, far_right, far_across = self.far
        first = list(range(self.over_z))
        last = list(range(self.over_z, 4))
        order = [(partner, p) for p in first[:2]] + [(s, p) for p in (last + first)[:2] for s in (left, right)]
        order += [(partner, p) for p in first[2:]] + [(s, p) for p in (last + first)[2:] for s in (left, right)]
        order += [(s, p) for p in first for s in (far_left, far_right)] + [(across, p) for p in last + first]
        order += [(far_across, p) for p in first]
        order += [(s, p) for s in (partner, far_left, far_right, far_across) for p in last]

        def targets_of(s, p):
            targets = []
            if s is partner and p < self.over_z:
                targets += [self.to_right, self.to_left]
            if s is left and p % 2 == 0 or s is far_left and p % 2 == 0 and p < self.over_z:
                targets.append(self.to_right)
            if s is right and p % 2 == 1 or s is far_right and p % 2 == 1 and p < self.over_z:
                targets.append(self.to_left)
            if p >= self.over_z and (s is left or s is right or s is across):
                targets.append(self.to_z)
            return targets

        plan = [(s, p, targets_of(s, p)) for s, p in order]

        def make(s, p, targets):
            def step():
                self.wait(s, p)
                for to in targets:
                    self.send(s, p, to)
            return step

        roles = {id(s): name for s, name in (
            (partner, "partner"), (left, "left"), (right, "right"), (across, "across"),
            (far_left, "far_left"), (far_right, "far_right"), (far_across, "far_across"),
        )}
        return {(roles[id(s)], p): make(s, p, targets) for s, p, targets in plan}

    def finish(self):
        for copy in self.copies:
            copy.wait_send()


class TreeScatter:
    def __init__(self, part, slots, send, recv, over_z):
        self.over_z = over_z
        first, last = range(over_z), range(over_z, 4)
        self.part, self.slots, self.send_sems, self.recv_sems = part, slots, send, recv
        self.d, self.t, self.x, self.z = place()
        d, x, z = self.d, self.x, self.z
        self.to_right = (d, tensor_index(lax.rem(x + 1, 4), z))
        self.to_left = (d, tensor_index(lax.rem(x + 3, 4), z))
        self.to_z = (d, tensor_index(x, 1 - z))
        names = [(kind, e, p) for e in (0, 1) for p in first for kind in ("relay", "right", "left")]
        names += [("z", 0, p) for p in first]
        names += [("zz", k, p) for k in range(4) for p in last]
        names += [(kind, 0, p) for p in last for kind in ("relay", "right", "left")]
        self.index = {name: n for n, name in enumerate(names)}
        self.copies = []

    def dest(self, k, e):
        z = self.z if e == 0 else 1 - self.z
        return tensor_index(lax.rem(self.x + k, 4), z)

    def stripe(self, p):
        return pl.ds(p * STRIPE, STRIPE)

    def send(self, k, e, p, to, name):
        n = self.index[name]
        copy = remote(
            self.part.at[self.dest(k, e), :, self.stripe(p)], self.slots.at[n], self.send_sems.at[len(self.copies)],
            self.recv_sems.at[n], to,
        )
        copy.start()
        self.copies.append(copy)

    def wait(self, name):
        n = self.index[name]
        slot = self.slots.at[n]
        remote(slot, slot, self.send_sems.at[0], self.recv_sems.at[n], self.to_z).wait_recv()

    def total(self, k, e, p, names):
        for name in names:
            self.wait(name)
        total = self.part[self.dest(k, e), :, self.stripe(p)].astype(f32)
        for name in names:
            total = total + self.slots[self.index[name]].astype(f32)
        return total

    def add(self, k, e, p, names):
        self.part[self.dest(k, e), :, self.stripe(p)] = self.total(k, e, p, names).astype(bf16)

    def begin_z(self, p):
        for k in (2, 1, 3, 0):
            self.send(k, 1, p, self.to_z, ("zz", k, p))

    def begin_x(self, e, p):
        if p % 2 == 0:
            self.send(2, e, p, self.to_left, ("relay", e, p))
            self.send(1, e, p, self.to_right, ("left", e, p))
        else:
            self.send(2, e, p, self.to_right, ("relay", e, p))
            self.send(3, e, p, self.to_left, ("right", e, p))

    def relay(self, e, p):
        if p % 2 == 0:
            self.add(3, e, p, [("relay", e, p)])
            self.send(3, e, p, self.to_left, ("right", e, p))
        else:
            self.add(1, e, p, [("relay", e, p)])
            self.send(1, e, p, self.to_right, ("left", e, p))

    def z_done(self, k, p):
        self.add(k, 0, p, [("zz", k, p)])

    def root_other(self, p):
        self.add(0, 1, p, [("right", 1, p), ("left", 1, p)])
        self.send(0, 1, p, self.to_z, ("z", 0, p))

    def result(self, p):
        names = [("right", 0, p), ("left", 0, p)]
        return self.total(0, 0, p, names + [("z", 0, p)] if p < self.over_z else names)

    def finish(self):
        for copy in self.copies:
            copy.wait_send()


class StageScatter:
    def __init__(self, part, core, ring, half, sems):
        self.part, self.core, self.ring, self.half = part, core, ring, half
        self.core_send, self.core_recv, self.ring_send, self.ring_recv, self.half_send, self.half_recv = sems
        d, t, _, _ = place()
        self.c, self.y, self.zh = lax.rem(d, 2), lax.rem(lax.div(d, 2), 4), lax.div(d, 8)
        self.to_core = (d + 1 - 2 * self.c, t)
        self.to_right = ((self.zh * 4 + lax.rem(self.y + 1, 4)) * 2 + self.c, t)
        self.to_left = ((self.zh * 4 + lax.rem(self.y + 3, 4)) * 2 + self.c, t)
        self.to_half = (((1 - self.zh) * 4 + self.y) * 2 + self.c, t)
        self.cut = core.shape[1] // 2
        self.copies = []

    def core_copy(self, j):
        return remote(
            self.part.at[2 * j + 1 - self.c], self.core.at[j], self.core_send.at[j], self.core_recv.at[j], self.to_core
        )

    def block(self, k, half):
        return 2 * (half * 4 + lax.rem(self.y + k, 4)) + self.c

    def fold_core(self, k, half):
        n = self.block(k, half)
        j = lax.div(n, 2)
        self.core_copy(j).wait_recv()
        self.part[n] = (self.part[n].astype(f32) + self.core[j].astype(f32)).astype(bf16)

    def rows(self, b):
        return pl.ds(b * self.cut, self.cut)

    def send(self, k, half, b, to, slot):
        copy = remote(
            self.part.at[self.block(k, half), self.rows(b)], self.ring.at[half, slot],
            self.ring_send.at[half, slot], self.ring_recv.at[half, slot], to,
        )
        copy.start()
        self.copies.append(copy)

    def wait(self, half, slot):
        ref = self.ring.at[half, slot]
        remote(ref, ref, self.ring_send.at[half, slot], self.ring_recv.at[half, slot], self.to_core).wait_recv()

    def begin_ring(self, half):
        self.fold_core(2, half)
        self.send(2, half, 0, self.to_left, 0)
        self.send(2, half, 1, self.to_right, 1)
        self.fold_core(1, half)
        self.send(1, half, 0, self.to_right, 2)
        self.fold_core(3, half)
        self.send(3, half, 1, self.to_left, 5)
        self.fold_core(0, half)

    def relay_ring(self, half):
        for k, b, slot, to, target in ((3, 0, 0, self.to_left, 4), (1, 1, 1, self.to_right, 3)):
            self.wait(half, slot)
            n = self.block(k, half)
            total = self.part[n, self.rows(b)].astype(f32) + self.ring[half, slot].astype(f32)
            self.part[n, self.rows(b)] = total.astype(bf16)
            self.send(k, half, b, to, target)

    def ring_total(self, half, b):
        total = self.part[self.block(0, half), self.rows(b)].astype(f32)
        for slot in (2 + b, 4 + b):
            self.wait(half, slot)
            total = total + self.ring[half, slot].astype(f32)
        return total

    def send_half(self):
        n = self.block(0, 1 - self.zh)
        for b in (0, 1):
            self.part[n, self.rows(b)] = self.ring_total(1 - self.zh, b).astype(bf16)
        copy = remote(self.part.at[n], self.half, self.half_send, self.half_recv, self.to_half)
        copy.start()
        self.half_copy = copy

    def result(self):
        totals = [self.ring_total(self.zh, b) for b in (0, 1)]
        self.half_copy.wait_recv()
        return [total + self.half[self.rows(b), :].astype(f32) for b, total in enumerate(totals)]

    def finish(self):
        for copy in self.copies:
            copy.wait_send()
        self.half_copy.wait_send()
        for j in range(8):
            self.core_copy(j).wait_send()


def kernel(
    source_ref, seg_ref, gain_ref, teacher_ref, branch_ref, hidden_ref, q_in, k_in, v_in, att_in, wq_in, wk_in,
    wv_in, w_out_in,
    dh_ref, gq_ref, gk_ref, gv_ref, gout_ref, ggain_ref, hidden_full,
    part, slope, slots, qkv_part, qkv_core, qkv_ring, qkv_half, out_part, out_core, out_ring, out_half,
    att_t, d_att, q_ref, k_ref, v_ref, cos_ref, sin_ref, seg_col, inv_own, inv_all, dk_acc, dv_acc,
    request, sources, gain_sum, gain_block, gain_tensor, gain_dp,
    source_send, source_recv, parcel_send, parcel_recv, hidden_send, hidden_recv, slope_send, slope_recv,
    inv_send, inv_recv, part_send, part_recv,
    qkv_core_send, qkv_core_recv, qkv_ring_send, qkv_ring_recv, qkv_half_send, qkv_half_recv,
    out_core_send, out_core_recv, out_ring_send, out_ring_recv, out_half_send, out_half_recv,
    gain_t_send, gain_t_recv, gain_d_send, gain_d_recv, load_sem, weight_sem, tile_sem,
):
    d, t, x, z = place()
    teacher, branch, own_hidden = part.at[0], part.at[1], part.at[2]
    dqkv = slope.at[:, :, pl.ds(0, 768)]
    dqkv_t = slope.at[pl.ds(0, 6), :, pl.ds(1024, 1024)]
    kept_hidden = slope.at[pl.ds(0, 4), :, pl.ds(2048, STRIPE)]
    tiles = slope.at[:, :, pl.ds(3072, 512)]

    loads = []

    def load(src, dst):
        copy = pltpu.make_async_copy(src, dst, load_sem.at[len(loads)])
        copy.start()
        loads.append(copy)
        return copy

    load_hidden = load(hidden_ref, own_hidden)
    load_teacher = load(teacher_ref, teacher)
    load_branch = load(branch_ref, branch)

    tensor_peers = [(d, lax.rem(t + k, N_TENSOR)) for k in range(1, N_TENSOR)]
    dp_peers = [(lax.rem(d + k, N_DP), t) for k in range(1, N_DP)]
    hidden_tree = TreeGather(hidden_ref, hidden_full, hidden_send, hidden_recv, 3)
    slope_tree = TreeGather(None, slope, slope_send, slope_recv, 2)
    tree = TreeScatter(part, slots, part_send, part_recv, 3)
    qkv = StageScatter(
        qkv_part, qkv_core, qkv_ring, qkv_half,
        (qkv_core_send, qkv_core_recv, qkv_ring_send, qkv_ring_recv, qkv_half_send.at[0], qkv_half_recv.at[0]),
    )
    out = StageScatter(
        out_part, out_core, out_ring, out_half,
        (out_core_send, out_core_recv, out_ring_send, out_ring_recv, out_half_send.at[0], out_half_recv.at[0]),
    )
    request[...] = jnp.broadcast_to(source_ref[...], (8, ROWS))
    greet(tensor_peers + dp_peers)

    def push_all(peers, src, dst, send, recv):
        copies = [remote(src, dst, send.at[k], recv.at[k], to) for k, to in enumerate(peers)]
        for copy in copies:
            copy.start()
        return copies

    source_copies = push_all(dp_peers, request, sources.at[d], source_send, source_recv)
    hidden_tree.begin()
    sources[d] = request[...]
    load_att = [load(att_in.at[pl.ds(s * ROWS, ROWS)], d_att.at[s]) for s in range(8)]
    load_w_out = [
        load(w_out_in.at[:, pl.ds(n * TILE, TILE)], qkv_part.at[n, pl.ds(0, 512)]) for n in range(16)
    ]
    load_qkv = [load(q_in, q_ref), load(k_in, k_ref), load(v_in, v_ref)]

    above = (
        lax.broadcasted_iota(jnp.int32, (ROWS, ROWS), 0) < lax.broadcasted_iota(jnp.int32, (ROWS, ROWS), 1)
    ).astype(bf16)
    block_row = lax.broadcasted_iota(jnp.int32, (SLOTS, ROWS), 0)
    chunk_ids = lax.shift_right_logical(block_row * 57, 9)
    slot_ids = block_row - CAPACITY * chunk_ids
    peer_ids = lax.broadcasted_iota(jnp.int32, (N_DP, ROWS), 0)
    row_ids = lax.broadcasted_iota(jnp.int32, (ROWS, ROWS), 0)

    def slot_onehot(mask, rank, q):
        return ((slot_ids == rank[q:q + 1]) & (mask[q:q + 1] > 0)).astype(f32).astype(bf16)

    def ranks(mask):
        return jnp.dot(mask.astype(bf16), above, preferred_element_type=f32).astype(jnp.int32)

    from_peer = (peer_ids == lax.shift_right_logical(source_ref[...], 10)).astype(f32)
    taken = jnp.sum(from_peer * (SLOTS * peer_ids + ranks(from_peer)).astype(f32), axis=0, keepdims=True)
    taken = jnp.concatenate([jnp.broadcast_to(taken, (ROWS, ROWS)).T] * 10, axis=1)
    lanes = lax.broadcasted_iota(jnp.int32, (ROWS, N_DP * SLOTS), 1).astype(f32)
    for k in range(8):
        onehot = (lanes == taken + CAPACITY * k).astype(f32).astype(bf16)
        for n in range(5):
            out_part[2 * n + k // 4, (k % 4) * ROWS:(k % 4 + 1) * ROWS, :] = onehot[:, n * TILE:(n + 1) * TILE]

    for copy in source_copies:
        copy.wait_recv()
    wanted = jnp.concatenate([sources[q, 0:1, :] for q in range(N_DP)], axis=0)
    mine = (lax.shift_right_logical(wanted, 10) == d).astype(f32)
    rank = ranks(mine)
    local_row = jnp.bitwise_and(wanted, ROWS - 1)
    picks = []
    for q in range(N_DP):
        row_onehot = (row_ids == local_row[q:q + 1]).astype(f32).astype(bf16)
        picks.append(lax.dot_general(slot_onehot(mine, rank, q), row_onehot, NT, preferred_element_type=f32))
    load_teacher.wait()
    chunks = jnp.concatenate([teacher[:, k * CHUNK:(k + 1) * CHUNK] for k in range(8)], axis=0)
    for b in range(4):
        pick = jnp.concatenate([
            jnp.concatenate([jnp.where(chunk_ids == k, picks[q], 0.0).astype(bf16) for k in range(8)], axis=1)
            for q in range(4 * b, 4 * b + 4)
        ], axis=0)
        values = jnp.dot(pick, chunks, preferred_element_type=f32).astype(bf16)
        for i in range(4):
            q = 4 * b + i
            part[3 + q // 8, :SLOTS, (q % 8) * CHUNK:(q % 8 + 1) * CHUNK] = values[i * SLOTS:(i + 1) * SLOTS]

    def slot_rows(first, q):
        columns = pl.ds(pl.multiple_of(lax.rem(q, 8) * CHUNK, CHUNK), CHUNK)
        return part.at[first + lax.div(q, 8), pl.ds(0, SLOTS), columns]

    parcel_copies = []
    for k, to in enumerate(dp_peers):
        copy = remote(slot_rows(3, to[0]), slot_rows(5, d), parcel_send.at[k], parcel_recv.at[k], to)
        copy.start()
        parcel_copies.append(copy)
    keep_own = load(slot_rows(3, d), slot_rows(5, d))

    load_hidden.wait()
    load_kept = load(own_hidden, hidden_full.at[t])
    squares = jnp.zeros((ROWS, 128), f32)
    for n in range(0, D, 128):
        values = own_hidden[:, n:n + 128].astype(f32)
        squares = squares + values * values
    inv_rms = lax.rsqrt(jnp.sum(squares, axis=1, keepdims=True) * (1.0 / D) + eps_norm)
    inv_own[...] = jnp.broadcast_to(inv_rms, (ROWS, 128))
    inv_copies = push_all(tensor_peers, inv_own, inv_all.at[t], inv_send, inv_recv)
    inv_all[t] = inv_own[...]

    hidden_steps = hidden_tree.steps()
    slope_steps = slope_tree.steps()

    def take(steps, *names):
        for role, p in names:
            steps.pop((role, p))()

    take(hidden_steps, ("partner", 0), ("left", 3), ("right", 3), ("left", 0))

    seg_row = seg_ref[...].astype(f32)
    before = jnp.zeros_like(seg_row)
    for value in range(3):
        count = jnp.sum((seg_row == value).astype(f32), axis=1, keepdims=True)
        before = before + jnp.where(seg_row > value, count, 0.0)
    positions = lax.broadcasted_iota(jnp.int32, (1, GROUP), 1).astype(f32) - before
    steps_down = lax.broadcasted_iota(jnp.int32, (HD // 2, 128), 0).astype(f32)
    frequency = jnp.exp(steps_down * float(-2.0 * np.log(theta_base) / HD))
    for n in range(0, GROUP, 128):
        angles = frequency * positions[:, n:n + 128]
        cos_ref[:, n:n + 128] = jnp.cos(angles)
        sin_ref[:, n:n + 128] = jnp.sin(angles)
    seg_col[...] = jnp.broadcast_to(seg_row, (128, GROUP)).T

    take(hidden_steps, ("partner", 1), ("right", 1))
    for copy in load_att:
        copy.wait()
    for e in (0, 1):
        rows = jnp.concatenate([d_att[2 * i + e] for i in range(4)], axis=0)
        att_t[e] = rows.astype(f32).T.astype(bf16)
    take(hidden_steps, ("left", 2))

    keep_own.wait()
    load_branch.wait()
    for copy in parcel_copies:
        copy.wait_recv()
    came = jnp.concatenate(
        [part[5 + q // 8, :SLOTS, (q % 8) * CHUNK:(q % 8 + 1) * CHUNK] for q in range(N_DP)], axis=0
    )
    for b in (0, 1):
        onehot = jnp.concatenate([out_part[2 * n + b] for n in range(5)], axis=1)
        target = jnp.dot(onehot, came, preferred_element_type=f32)
        for i in range(4):
            columns = slice((4 * b + i) * CHUNK, (4 * b + i + 1) * CHUNK)
            change = branch[:, columns].astype(f32) - target[i * ROWS:(i + 1) * ROWS]
            slope[t, :, columns] = (change * (N_DP * GROUP) ** -0.5).astype(bf16)
    slope_tree.begin()
    for copy in parcel_copies:
        copy.wait_send()

    for copy in load_qkv:
        copy.wait()
    blk = 256
    scale = HD ** -0.5

    def forward(i):
        rows = slice(i * blk, (i + 1) * blk)
        seen = (i + 1) * blk
        keys = jnp.concatenate([seg_col[:seen, :]] * 2, axis=1)
        allowed = (keys == seg_row[:, rows]) & (
            lax.broadcasted_iota(jnp.int32, (seen, blk), 0) <= lax.broadcasted_iota(jnp.int32, (seen, blk), 1) + i * blk
        )
        for h in range(4):
            scores = lax.dot_general(
                k_ref[:seen, :], q_ref[rows, h * HD:(h + 1) * HD], NT, preferred_element_type=f32
            ) * scale
            scores = jnp.where(allowed, scores, -1e30)
            weights = jnp.where(allowed, jnp.exp(scores - jnp.max(scores, axis=0, keepdims=True)), 0.0)
            soft = (weights * (1.0 / jnp.sum(weights, axis=0, keepdims=True))).astype(bf16)
            first = (4 * i + h) * blk
            part[:2 * (i + 1), :, first:first + blk] = soft.reshape(2 * (i + 1), ROWS, blk)

    load_kept.wait()
    take(hidden_steps, ("far_left", 0), ("far_right", 1), ("across", 3))
    forward(0)
    take(slope_steps, ("partner", 0), ("partner", 1))
    forward(1)
    take(slope_steps, ("left", 2), ("right", 3), ("left", 3), ("right", 2))
    forward(2)
    take(slope_steps, ("left", 0), ("right", 1))
    take(hidden_steps, ("partner", 2))
    take(slope_steps, ("far_left", 0), ("far_right", 1))
    take(slope_steps, ("across", 2), ("across", 3))
    forward(3)

    take(slope_steps, ("across", 0), ("across", 1), ("left", 1), ("right", 0))
    take(hidden_steps, ("far_left", 2))
    for copy in load_w_out:
        copy.wait()

    def slope_rows(e, columns):
        return jnp.concatenate([slope[2 * i + e, :, columns] for i in range(4)], axis=0)

    def attended_slope(e):
        def tile(n, carry):
            heads = pl.ds(pl.multiple_of(n * 256, 256), 256)
            value = jnp.zeros((512, 256), f32)
            for k in range(16):
                rows = slope_rows(e, slice(k * TILE, (k + 1) * TILE))
                value += lax.dot_general(rows, qkv_part[k, heads, :], NT, preferred_element_type=f32)
            value = value.astype(bf16)
            for i in range(4):
                d_att[2 * i + e, :, heads] = value[i * ROWS:(i + 1) * ROWS]
            return carry

        lax.fori_loop(0, 2, tile, 0)

    def out_gradient(e, first):
        def tile(n, carry):
            columns = pl.ds(pl.multiple_of(n * TILE, TILE), TILE)
            value = jnp.dot(att_t[e], slope_rows(e, columns), preferred_element_type=f32)
            if not first:
                value = value + out_part[n].astype(f32)
            out_part[n] = value.astype(bf16)
            return carry

        return tile

    attended_slope(z)
    lax.fori_loop(0, 16, out_gradient(z, True), 0)
    for step in slope_steps.values():
        step()
    attended_slope(1 - z)
    weight_copies = []
    for n in range(16):
        rows = pl.ds(n * TILE, TILE)
        for i, (src, dst) in enumerate((
            (wq_in.at[rows, pl.ds(0, 256)], qkv_part.at[n, pl.ds(0, 256)]),
            (wq_in.at[rows, pl.ds(256, 256)], qkv_part.at[n, pl.ds(256, 256)]),
            (wk_in.at[rows], qkv_part.at[n, pl.ds(512, 256), pl.ds(0, 128)]),
            (wv_in.at[rows], qkv_part.at[n, pl.ds(512, 256), pl.ds(128, 128)]),
        )):
            copy = pltpu.make_async_copy(src, dst, weight_sem.at[n, i])
            copy.start()
            weight_copies.append(copy)
    slope_tree.finish()
    lax.fori_loop(0, 16, out_gradient(1 - z, False), 0)
    for j in range(8):
        out.core_copy(j).start()
    for p in range(4):
        load(hidden_ref.at[:, pl.ds(p * STRIPE, STRIPE)], kept_hidden.at[p])

    dk_acc[...] = jnp.zeros_like(dk_acc)
    dv_acc[...] = jnp.zeros_like(dv_acc)
    k_t = k_ref[...].astype(f32).T.astype(bf16)

    def rotate_back(values, columns):
        u, w = values[:64], values[64:]
        c, s = cos_ref[:, columns], sin_ref[:, columns]
        return jnp.concatenate([u * c + w * s, w * c - u * s], axis=0)

    for i in range(GROUP // blk):
        rows = slice(i * blk, (i + 1) * blk)
        seen = (i + 1) * blk
        for h in range(4):
            cols = slice(h * HD, (h + 1) * HD)
            q = q_ref[rows, cols]
            da = d_att[2 * i:2 * i + 2, :, cols].reshape(blk, HD)
            first = (4 * i + h) * blk
            probs = part[:2 * (i + 1), :, first:first + blk].reshape(seen, blk)
            soft = probs.astype(f32)
            d_probs = lax.dot_general(v_ref[:seen, :], da, NT, preferred_element_type=f32)
            delta = jnp.sum(soft * d_probs, axis=0, keepdims=True)
            d_scores = (soft * (d_probs - delta) * scale).astype(bf16)
            dv_acc[:seen, :] += jnp.dot(probs, da, preferred_element_type=f32)
            dk_acc[:seen, :] += jnp.dot(d_scores, q, preferred_element_type=f32)
            dq_t = rotate_back(jnp.dot(k_t[:, :seen], d_scores, preferred_element_type=f32), rows)
            dqkv_t[h, :, rows] = dq_t.astype(bf16)
            dqkv[2 * i:2 * i + 2, :, cols] = dq_t.T.astype(bf16).reshape(2, ROWS, HD)
        if i == 1:
            out.begin_ring(0)
            out.begin_ring(1)
    dk_t = rotate_back(dk_acc[...].T, slice(0, GROUP))
    dqkv_t[4] = dk_t.astype(bf16)
    dqkv[:, :, 512:640] = dk_t.T.astype(bf16).reshape(8, ROWS, HD)
    dqkv_t[5] = dv_acc[...].T.astype(bf16)
    dqkv[:, :, 640:768] = dv_acc[...].astype(bf16).reshape(8, ROWS, HD)
    out.relay_ring(0)
    out.relay_ring(1)

    for step in hidden_steps.values():
        step()
    for copy in inv_copies:
        copy.wait_recv()
    for copy in weight_copies:
        copy.wait()

    def tile_copy(n, slot):
        columns = pl.ds(pl.multiple_of(n * TILE, TILE), TILE)
        return pltpu.make_async_copy(hidden_full.at[:, :, columns], tiles.at[:, :, pl.ds(pl.multiple_of(slot * TILE, TILE), TILE)], tile_sem.at[slot])

    order = (0, 1, 3, 2)
    tile_copy(4 * order[0], 0).start()
    for g, p in enumerate(order):
        following = order[g + 1] if g < 3 else None

        def tile(i, carry, p=p, following=following):
            n = 4 * p + i
            slot = lax.rem(i, 2)
            if following is None:
                @pl.when(i < 3)
                def _():
                    tile_copy(n + 1, 1 - slot).start()
            else:
                tile_copy(n + 1 + lax.div(i + 1, 4) * (4 * (following - p) - 4), 1 - slot).start()
            tile_copy(n, slot).wait()
            columns = pl.ds(pl.multiple_of(n * TILE, TILE), TILE)
            inv = inv_all[...].reshape(GROUP, 128)
            held = tiles[:, :, pl.ds(pl.multiple_of(slot * TILE, TILE), TILE)]
            unit = held.reshape(GROUP, TILE).astype(f32) * jnp.concatenate([inv, inv], axis=1)
            normed = (unit * gain_ref[:, columns]).astype(bf16)
            grads = dqkv[...].reshape(GROUP, 768)
            total = lax.dot_general(grads[:, :256], qkv_part[n, :256, :], NT, preferred_element_type=f32)
            total += lax.dot_general(grads[:, 256:512], qkv_part[n, 256:512, :], NT, preferred_element_type=f32)
            total += lax.dot_general(grads[:, 512:], qkv_part[n, 512:, :], NT, preferred_element_type=f32)
            part[:, :, columns] = total.astype(bf16).reshape(8, ROWS, TILE)
            gain_sum[:, columns] = jnp.sum((total * unit).reshape(ROWS, 8, TILE), axis=0)
            qkv_part[n] = jnp.dot(
                dqkv_t[...].reshape(768, GROUP), normed, preferred_element_type=f32
            ).astype(bf16)
            return carry

        lax.fori_loop(0, 4, tile, 0)
        if p >= tree.over_z:
            tree.begin_z(p)
        else:
            tree.begin_x(1, p)
            tree.begin_x(0, p)
        qkv.core_copy(2 * p).start()
        qkv.core_copy(2 * p + 1).start()
        if g == 1:
            out.send_half()
        if g == 2:
            qkv.begin_ring(0)

    gain_row = jnp.sum(gain_sum[...], axis=0, keepdims=True)
    for i in range(32):
        gain_block[0, i:i + 1, :] = gain_row[:, i * 128:(i + 1) * 128]
    gain_tensor[t] = gain_block[0]
    gain_copies = push_all(tensor_peers, gain_block.at[0], gain_tensor.at[t], gain_t_send, gain_t_recv)

    tree.relay(1, 0)
    tree.relay(0, 0)
    tree.z_done(2, 3)
    qkv.begin_ring(1)
    qkv.relay_ring(0)
    tree.z_done(1, 3)

    for copy in gain_copies:
        copy.wait_recv()
    gain_total = gain_tensor[0]
    for k in range(1, N_TENSOR):
        gain_total = gain_total + gain_tensor[k]
    gain_block[1] = gain_total
    gain_dp[d] = gain_total
    dp_copies = push_all(dp_peers, gain_block.at[1], gain_dp.at[d], gain_d_send, gain_d_recv)

    tree.relay(1, 1)
    tree.relay(0, 1)
    tree.z_done(3, 3)
    tree.begin_x(0, 3)
    qkv.relay_ring(1)
    tree.z_done(0, 3)
    tree.root_other(0)
    qkv.send_half()
    tree.relay(1, 2)
    tree.relay(0, 2)
    tree.root_other(1)
    tree.relay(0, 3)
    tree.root_other(2)
    for b, value in enumerate(out.result()):
        gout_ref[b * 256:(b + 1) * 256, :] = value

    for copy in dp_copies:
        copy.wait_recv()
    gain_total = gain_dp[0]
    for k in range(1, N_DP):
        gain_total = gain_total + gain_dp[k]
    ggain_ref[...] = gain_total

    top, bottom = qkv.result()
    gq_ref[:, :384] = top.T
    gq_ref[:, 384:] = bottom[:128].T
    gk_ref[...] = bottom[128:256].T
    gv_ref[...] = bottom[256:].T

    for copy in loads[-4:]:
        copy.wait()
    inv = inv_own[:, 0:1]
    dots = jnp.zeros((ROWS, 1), f32)
    for p in (0, 1, 3, 2):
        columns = slice(p * STRIPE, (p + 1) * STRIPE)
        scaled = tree.result(p) * gain_ref[:, columns]
        dh_ref[:, columns] = scaled
        unit = kept_hidden[p].astype(f32) * inv
        dots = dots + jnp.sum(scaled * unit, axis=1, keepdims=True)
    mean = dots * (1.0 / D)
    for p in range(4):
        columns = slice(p * STRIPE, (p + 1) * STRIPE)
        unit = kept_hidden[p].astype(f32) * inv
        dh_ref[:, columns] = inv * (dh_ref[:, columns] - unit * mean)

    hidden_tree.finish()
    tree.finish()
    out.finish()
    qkv.finish()
    for copy in source_copies + inv_copies + gain_copies + dp_copies:
        copy.wait_send()


def hand_over(*refs):
    sources, results, held, sems = refs[:6], refs[6:12], refs[12:18], refs[18]
    loads = [pltpu.make_async_copy(sources[i], held[i], sems.at[0, i]) for i in range(6)]
    stores = [pltpu.make_async_copy(held[i], results[i], sems.at[1, i]) for i in range(6)]
    for copy in loads:
        copy.start()
    for before, after in zip(loads, stores):
        before.wait()
        after.start()
    for copy in stores:
        copy.wait()


def per_device(
    hidden_in, teacher, row_source, segments, branch, queries, key_rot, value_rows, attended, norm_gain,
    w_query, w_key, w_value, w_out,
):
    any_space = pl.BlockSpec(memory_space=pl.ANY)
    vmem = pl.BlockSpec(memory_space=pltpu.VMEM)
    dma = pltpu.SemaphoreType.DMA
    scratch = pltpu.VMEM
    stage_sems = [dma((8,)), dma((8,)), dma((2, 6)), dma((2, 6)), dma((1,)), dma((1,))]
    shape = jax.ShapeDtypeStruct
    *results, _ = pl.pallas_call(
        kernel,
        out_shape=(
            shape((ROWS, D), f32), shape((256, 512), f32), shape((256, 128), f32), shape((256, 128), f32),
            shape((512, 256), f32), shape((32, 128), f32), shape((N_TENSOR, ROWS, D), bf16),
        ),
        in_specs=[vmem] * 3 + [any_space] * 11,
        out_specs=(vmem,) * 6 + (any_space,),
        scratch_shapes=[
            scratch((8, ROWS, D), bf16), scratch((8, ROWS, D), bf16), scratch((28, ROWS, STRIPE), bf16),
            scratch((16, 768, 256), bf16), scratch((8, 768, 256), bf16), scratch((2, 6, 384, 256), bf16), scratch((768, 256), bf16),
            scratch((16, 512, 256), bf16), scratch((8, 512, 256), bf16), scratch((2, 6, 256, 256), bf16), scratch((512, 256), bf16),
            scratch((2, 512, 512), bf16), scratch((8, ROWS, 512), bf16),
            scratch((GROUP, 512), bf16), scratch((GROUP, HD), bf16), scratch((GROUP, HD), bf16),
            scratch((HD // 2, GROUP), f32), scratch((HD // 2, GROUP), f32), scratch((GROUP, 128), f32),
            scratch((ROWS, 128), f32), scratch((N_TENSOR, ROWS, 128), f32),
            scratch((GROUP, HD), f32), scratch((GROUP, HD), f32),
            scratch((8, ROWS), jnp.int32), scratch((N_DP, 8, ROWS), jnp.int32),
            scratch((8, D), f32), scratch((2, 32, 128), f32), scratch((N_TENSOR, 32, 128), f32), scratch((N_DP, 32, 128), f32),
            dma((15,)), dma((15,)), dma((15,)), dma((15,)),
            dma((28,)), dma((8, 4)), dma((28,)), dma((8, 4)),
            dma((7,)), dma((7,)), dma((28,)), dma((28,)),
        ] + stage_sems + stage_sems + [
            dma((7,)), dma((7,)), dma((15,)), dma((15,)), dma((40,)), dma((16, 4)), dma((2,)),
        ],
        compiler_params=pltpu.CompilerParams(
            collective_id=1, has_side_effects=True, vmem_limit_bytes=60 * 2**20
        ),
        cost_estimate=pl.CostEstimate(flops=27 * 10**9, bytes_accessed=60 * 2**20, transcendentals=4 * 2**20),
    )(
        row_source[None, :], segments, norm_gain[None, :], teacher, branch, hidden_in, queries, key_rot, value_rows,
        attended, w_query, w_key, w_value, w_out,
    )
    d_hidden, grad_query, grad_key, grad_value, grad_out, grad_gain = pl.pallas_call(
        hand_over,
        out_shape=[shape(value.shape, value.dtype) for value in results],
        in_specs=[any_space] * 6,
        out_specs=[any_space] * 6,
        scratch_shapes=[scratch(value.shape, value.dtype) for value in results] + [dma((2, 6))],
        compiler_params=pltpu.CompilerParams(vmem_limit_bytes=60 * 2**20),
    )(*results)
    return (grad_query, grad_key, grad_value, grad_out, grad_gain.reshape(D), d_hidden)


def solution(mesh):
    return jax.shard_map(
        per_device,
        mesh=mesh,
        in_specs=(
            P(("dp", "tensor"), None),
            P(("dp", "tensor"), None),
            P(("dp", "tensor")),
            P("dp", None),
            P(("dp", "tensor"), None),
            P("dp", "tensor"),
            P("dp", "tensor"),
            P("dp", "tensor"),
            P("dp", "tensor"),
            P(),
            P(None, "tensor"),
            P(None, "tensor"),
            P(None, "tensor"),
            P("tensor", None),
        ),
        out_specs=(
            P("dp", "tensor"),
            P("dp", "tensor"),
            P("dp", "tensor"),
            P("tensor", "dp"),
            P(),
            P(("dp", "tensor"), None),
        ),
        check_vma=False,
    )
```
